128 devices in a mesh: section: 2 (over core), expert: 16 (over y, z), dp: 4 (over x).
Axes of the slice: x: 4, y: 4, z: 4, core: 2. Of those that a mesh axis runs over, the one named last changes fastest.
Arguments:
- inputs: bfloat16 [2, 9600, 512], P(None, ('expert', 'dp')), may hold values from -16 to 16
- cotangent: bfloat16 [2, 9600, 512], P(None, ('expert', 'dp')), may hold values from -6 to 6
- norm_gains: float32 [2, 2, 512], P('section'), may hold values from 0.25 to 1.75
- norm_biases: float32 [2, 2, 512], P('section'), may hold values from -1.2 to 1.2
- w_qkv: bfloat16 [2, 512, 1536], P('section'), may hold values from -0.375 to 0.375
- w_attn_out: bfloat16 [2, 512, 512], P('section'), may hold values from -0.75 to 0.75
- w_router: bfloat16 [2, 512, 16], P('section'), may hold values from -0.1875 to 0.1875
- w_expert_in: bfloat16 [2, 16, 512, 2048], P('section', 'expert', None, 'dp'), may hold values from -0.25 to 0.25
- w_expert_out: bfloat16 [2, 16, 2048, 512], P('section', 'expert', 'dp'), may hold values from -0.25 to 0.25
- routes: int32 [2, 2, 9600, 2], P('section', None, ('expert', 'dp')), may hold values from 0 to 15, all different within a row; in each aligned block of 150 rows (0 to 149, 150 to 299, ..., all dimensions but the last counted through in order) at most 24 rows name the same one
Outputs:
- layer_outputs: bfloat16 [2, 2, 9600, 512], P('section', None, ('expert', 'dp'))
- layer_input_grads: bfloat16 [2, 2, 9600, 512], P('section', None, ('expert', 'dp'))
- grad_norm_gains: float32 [2, 2, 512], P('section', None, ('expert', 'dp'))
- grad_norm_biases: float32 [2, 2, 512], P('section', None, ('expert', 'dp'))
- grad_qkv: float32 [2, 512, 1536], P('section', ('expert', 'dp'))
- grad_attn_out: float32 [2, 512, 512], P('section', ('expert', 'dp'))
- grad_router: float32 [2, 512, 16], P('section', ('expert', 'dp'))
- grad_expert_in: float32 [2, 16, 512, 2048], P('section', 'expert', None, 'dp')
- grad_expert_out: float32 [2, 16, 2048, 512], P('section', 'expert', 'dp')
The draws below stay inside these ranges and needn't reach their ends.
Inputs may be any that keep to these rules, and one draw needn't show every extreme that they name: `routes`: in each aligned block of 150 rows (one device's tokens of one layer and micro-batch) the two entries of a row differ and no expert is named by more than 24 entries.
All inputs are finite; a program needn't handle non-finite values.
Results may differ from the reference program's by a relative error of at most 0.033.
Values may be sent and summed in bfloat16 or wider, within the bound.
A program may use at most 192 MiB of HBM per device.

```python
import math
from functools import partial
import jax
import jax.numpy as jnp
import numpy as np
from jax import lax

D = 512
HEADS = 8
HEAD_DIM = 64
FF = 2048
SEQ = 50
MICRO = 2
LAYERS = 2
EXPERTS = 16
TOK_DEV = 150
TOKENS = 9600
CAP = 24


def raised(values, stream_key, source, target, parts, factor):
    owner, partner = [(jnp.arange(values.shape[axis_at]) // (values.shape[axis_at] // parts)).reshape([-1 if axis == axis_at else 1 for axis in range(values.ndim)]) for axis_at in (source, target)]
    chosen = jax.random.permutation(stream_key, parts)[partner]
    strong = (owner == chosen) | (owner == (partner + parts // 2) % parts)
    return jnp.where(strong, factor * values, values)


def block_scale(key, shape, cuts, least, top_value):
    level = 1.0
    for dim, parts in cuts:
        draws = jax.random.uniform(jax.random.fold_in(jax.random.fold_in(key, 6), dim), (parts,), jnp.float32, least / len(cuts), top_value / len(cuts))
        level = level * jnp.repeat(jnp.exp(draws), shape[dim] // parts).reshape((-1,) + (1,) * (len(shape) - 1 - dim))
    return level


def shared_out(stream_key, own, number, rows, number_of, top, bound, slope):
    ranking = jax.random.permutation(stream_key, number_of)
    crowded, ordinary = portions_of(number_of, rows * top, bound, slope, True), portions_of(number_of, rows * top, bound, slope, False)
    places = jnp.arange(number_of)

    def named(sizes, turn):
        used = int((sizes > 0).sum())
        fixed = max(1, used // 4)
        passed = fixed + (places - fixed + turn * (used - fixed)) % max(1, number_of - fixed)
        return jnp.zeros((number_of,), jnp.int32).at[ranking[jnp.where(places < fixed, places, passed)]].set(jnp.asarray(sizes, jnp.int32))

    sizes = jnp.where(number % 4 == 0, named(crowded, number // 4), named(ordinary, number - number // 4 - 1))
    mixed = jax.random.permutation(jax.random.fold_in(own, 3), number_of)
    giver, receiver = mixed[0:number_of // 2 * 2:2], mixed[1:number_of // 2 * 2:2]
    slack = jnp.minimum(sizes[giver] - 1, bound - sizes[receiver]) // 2
    slack = jnp.where((giver == ranking[0]) | (receiver == ranking[0]) | (sizes[receiver] == 0), 0, jnp.maximum(slack, 0))
    passed = jax.random.randint(jax.random.fold_in(own, 4), (number_of // 2,), 0, 1 << 20) % (slack + 1)
    sizes = sizes.at[giver].add(-passed).at[receiver].add(passed)
    labels = jnp.searchsorted(jnp.cumsum(sizes), jnp.arange(rows * top), side="right").astype(jnp.int32)
    listing = labels.reshape(top, rows).T
    listing = listing[jax.random.permutation(jax.random.fold_in(own, 1), rows)]
    turn = jax.random.randint(jax.random.fold_in(own, 2), (rows, 1), 0, top)
    return jnp.take_along_axis(listing, (jnp.arange(top)[None, :] + turn) % top, axis=1)


def portions_of(amount, total, bound, lean, full):
    portions = [(1 << 20) // math.isqrt(rank ** lean) + 1 for rank in range(1, amount + 1)]
    largest = bound if full else min(bound, max(-(-total // amount), total * portions[0] // sum(portions)))
    least = 1 if total - largest >= amount - 1 else 0
    given, surplus = [largest] + [least] * (amount - 1), total - largest - least * (amount - 1)
    while surplus > 0:
        candidates = [i for i in range(1, amount) if given[i] < largest] or [i for i in range(1, amount) if given[i] < bound]
        pool, left = sum([portions[i] for i in candidates]), surplus
        for i in candidates:
            more = min(bound - given[i], max(1, left * portions[i] // pool), surplus)
            given[i] = given[i] + more
            surplus = surplus - more
    return np.array(given)


def gaussian(own_key, extent, scale, reach, split=(), kind=jnp.bfloat16):
    entries = jax.random.normal(own_key, extent, jnp.float32) * scale
    if len(split) > 0:
        entries = block_scale(own_key, extent, split, -0.22, 0.18) * entries
    return jnp.clip(entries, min=-reach, max=reach).astype(kind)


def heavy_noise(key, extent, scale, most, shards, heavy, kind=jnp.bfloat16):
    entries = scale * jax.random.normal(key, extent, jnp.float32)
    if shards:
        entries = entries * block_scale(key, extent, shards, -0.22, 0.18)
    return jnp.clip(raised(entries, jax.random.fold_in(key, 3), *heavy), -most, most).astype(kind)


def setup_inputs(seed: int = 0) -> dict:
    seeds = jax.random.split(jax.random.key(seed), 11)
    inputs = heavy_noise(seeds[0], (MICRO, TOKENS, D), 1.0, 16.0, ((1, 64),), (1, 2, 64, 4.0))
    cotangent = gaussian(seeds[1], (MICRO, TOKENS, D), 1.0, 6.0, ((1, 64),))
    norm_gains = jnp.clip(1.0 + 0.15 * jax.random.normal(seeds[2], (LAYERS, 2, D), jnp.float32), 0.25, 1.75)
    norm_biases = gaussian(seeds[3], (LAYERS, 2, D), 0.2, 1.2, ((0, 2),), jnp.float32)
    w_qkv = gaussian(seeds[4], (LAYERS, D, 3 * D), (D // 2) ** -0.5, 0.375, ((0, 2),))
    w_attn_out = gaussian(seeds[5], (LAYERS, D, D), (D // 8) ** -0.5, 0.75, ((0, 2),))
    w_router = gaussian(seeds[6], (LAYERS, D, EXPERTS), (2 * D) ** -0.5, 0.1875, ((0, 2),))
    w_expert_in = gaussian(seeds[7], (LAYERS, EXPERTS, D, FF), D ** -0.5, 0.25, ((0, 2), (1, 16), (3, 4)))
    w_expert_out = gaussian(seeds[8], (LAYERS, EXPERTS, FF, D), (FF // 4) ** -0.5, 0.25, ((0, 2), (1, 16), (2, 4)))
    routes_keys = jax.random.split(jax.random.fold_in(seeds[9], 1), LAYERS * MICRO * TOKENS // TOK_DEV)
    routes_turns = jax.random.permutation(jax.random.fold_in(seeds[9], 3), LAYERS * MICRO * TOKENS // TOK_DEV)
    routes = jax.vmap(lambda own, number: shared_out(jax.random.fold_in(seeds[9], 2), own, number, TOK_DEV, EXPERTS, 2, CAP, 1))(routes_keys, routes_turns).reshape((LAYERS, MICRO, TOKENS, 2))
    return {"inputs": inputs, "cotangent": cotangent, "norm_gains": norm_gains, "norm_biases": norm_biases, "w_qkv": w_qkv, "w_attn_out": w_attn_out, "w_router": w_router, "w_expert_in": w_expert_in, "w_expert_out": w_expert_out, "routes": routes}


HIGHEST = lax.Precision.HIGHEST
EPSILON = 1e-06

@jax.custom_vjp
def low(v):
    return lax.optimization_barrier(v.astype(jnp.bfloat16)).astype(jnp.float32)

@jax.custom_vjp
def low_back(v):
    return v

def low_keep(v):
    return (low(v), None)

def low_pass(kept, grad):
    return (grad,)

def back_keep(v):
    return (v, None)

def back_low(kept, grad):
    return (low(grad),)
low.defvjp(low_keep, low_pass)
low_back.defvjp(back_keep, back_low)

def norm_apply(values, norm_gain, offset):
    center = values - lax.optimization_barrier(jnp.mean(values, -1, keepdims=True))
    spread = lax.optimization_barrier(jnp.mean(center * center, -1, keepdims=True))
    return center * lax.rsqrt(spread + EPSILON) * norm_gain + offset

def slot_rows(chosen):
    blocks = chosen.shape[0]
    flattened = chosen.reshape(blocks, -1)
    matches = (flattened[:, :, None] == jnp.arange(EXPERTS, dtype=jnp.int32)).astype(jnp.int32)
    running = jnp.cumsum(matches, axis=1, dtype=jnp.int32)
    position = lax.optimization_barrier(jnp.sum(running * matches, axis=2, dtype=jnp.int32)) - 1
    return position.reshape(chosen.shape).astype(jnp.int32)

def gate_values(logits, chosen):
    picked = jnp.take_along_axis(jax.nn.softmax(logits, axis=-1), chosen, axis=1)
    return picked / lax.optimization_barrier(jnp.sum(picked, axis=1, keepdims=True))

def layer(params, states, chosen):
    gains, biases, qkv_weight, out_weight, router_weight, expert_in, expert_out = params
    tokens = states.shape[0]
    images = tokens // SEQ
    normed = low(norm_apply(states, gains[0], biases[0]))
    packed = low_back(low(jnp.dot(normed, qkv_weight, precision=HIGHEST)))
    packed = packed.reshape(images, SEQ, 3, HEADS, HEAD_DIM)
    queries = packed[:, :, 0]
    key_rows = packed[:, :, 1]
    value_rows = packed[:, :, 2]
    scores = jnp.einsum('bqhd,bkhd->bhqk', queries, key_rows, precision=HIGHEST) * HEAD_DIM ** (-0.5)
    scores = low_back(scores)
    shares = low(jax.nn.softmax(scores, axis=-1))
    blended = jnp.einsum('bhqk,bkhd->bqhd', shares, value_rows, precision=HIGHEST).reshape(tokens, D)
    blended = low_back(low(blended))
    attended = states + low_back(jnp.dot(blended, out_weight, precision=HIGHEST))
    normed_two = low(norm_apply(attended, gains[1], biases[1]))
    logits = jnp.dot(normed_two, router_weight, precision=HIGHEST)
    gates = gate_values(logits, chosen)
    sources = tokens // TOK_DEV
    position = slot_rows(chosen.reshape(sources, TOK_DEV, 2)).reshape(tokens, 2)
    source_index = (jnp.arange(tokens, dtype=jnp.int32) // TOK_DEV)[:, None]
    target = (chosen * (sources * CAP) + source_index * CAP + position).astype(jnp.int32)
    copies = low_back(jnp.broadcast_to(normed_two[:, None, :], (tokens, 2, D)))
    buffer = jnp.zeros((EXPERTS * sources * CAP, D), jnp.float32)
    buffer = buffer.at[target.reshape(-1)].set(copies.reshape(-1, D)).reshape(EXPERTS, sources * CAP, D)
    before = low_back(jnp.einsum('erd,edf->erf', buffer, expert_in, precision=HIGHEST))
    hidden = low(jax.nn.gelu(before, approximate=False))
    result = low_back(low(jnp.einsum('erf,efd->erd', hidden, expert_out, precision=HIGHEST)))
    picked = result.reshape(-1, D)[target]
    return attended + lax.optimization_barrier(jnp.sum(gates[:, :, None] * picked, axis=1))

def reference(inputs, cotangent, norm_gains, norm_biases, w_qkv, w_attn_out, w_router, w_expert_in, w_expert_out, routes):
    stacks = (norm_gains.astype(jnp.float32), norm_biases.astype(jnp.float32), w_qkv.astype(jnp.float32), w_attn_out.astype(jnp.float32), w_router.astype(jnp.float32), w_expert_in.astype(jnp.float32), w_expert_out.astype(jnp.float32))
    totals = [tuple((jnp.zeros_like(member[layer_no]) for member in stacks)) for layer_no in range(LAYERS)]
    made = []
    returned = []
    for micro_no in range(MICRO):
        current = inputs[micro_no].astype(jnp.float32)
        backs = []
        outs_here = []
        for layer_no in range(LAYERS):
            params = tuple((member[layer_no] for member in stacks))
            result, back = jax.vjp(partial(layer, chosen=routes[layer_no, micro_no]), params, current)
            current = low(result)
            outs_here.append(current)
            backs.append(back)
        gradient = cotangent[micro_no].astype(jnp.float32)
        grads_here = [gradient for layer_no in range(LAYERS)]
        for layer_no in reversed(range(LAYERS)):
            param_grads, gradient = backs[layer_no](gradient)
            gradient = low(gradient)
            grads_here[layer_no] = gradient
            totals[layer_no] = tuple((first + second for first, second in zip(totals[layer_no], param_grads)))
        made.append(jnp.stack(outs_here))
        returned.append(jnp.stack(grads_here))
    layer_outputs = jnp.stack(made, 1).astype(jnp.bfloat16)
    layer_input_grads = jnp.stack(returned, 1).astype(jnp.bfloat16)
    stacked = [jnp.stack([totals[layer_no][member] for layer_no in range(LAYERS)]) for member in range(7)]
    return (layer_outputs, layer_input_grads, stacked[0], stacked[1], stacked[2], stacked[3], stacked[4], stacked[5], stacked[6])
```

```python
from functools import partial

import jax
import jax.numpy as jnp
from jax import lax
from jax.experimental import pallas as pl
from jax.experimental.pallas import tpu as pltpu
from jax.sharding import PartitionSpec as P

HEADS = 8
HEAD_DIM = 64
SEQ = 50
ROWS = 64
EPSILON = 1e-06
MESH = pl.DeviceIdType.MESH
F32 = jnp.float32
BF16 = jnp.bfloat16
EXTRA = 128


def nn(a, b):
    return lax.dot_general(a, b, (((1,), (0,)), ((), ())), preferred_element_type=F32)


def nt(a, b):
    return lax.dot_general(a, b, (((1,), (1,)), ((), ())), preferred_element_type=F32)


def tn(a, b):
    return lax.dot_general(a, b, (((0,), (0,)), ((), ())), preferred_element_type=F32)


def iota(shape, dim):
    return lax.broadcasted_iota(jnp.int32, shape, dim)


def split_sum(values):
    high = values.astype(BF16)
    return high, (values - high.astype(F32)).astype(BF16)


def normalized(values):
    center = values - jnp.mean(values, axis=-1, keepdims=True)
    root = lax.rsqrt(jnp.mean(center * center, axis=-1, keepdims=True) + EPSILON)
    return center * root, root


def norm_back(grad, norm, root, gain):
    scaled = grad * gain
    return root * (
        scaled
        - jnp.mean(scaled, axis=-1, keepdims=True)
        - norm * jnp.mean(scaled * norm, axis=-1, keepdims=True)
    )


def gelu_parts(x):
    z = jnp.abs(x) * 0.7071067811865476
    t = 1.0 / (1.0 + 0.3275911 * z)
    poly = t * (
        0.254829592 + t * (-0.284496736 + t * (1.421413741 + t * (-1.453152027 + t * 1.061405429)))
    )
    bell = jnp.exp(-z * z)
    tail = 0.5 * poly * bell
    share = jnp.where(x >= 0.0, 1.0 - tail, tail)
    return x * share, share + x * bell * 0.3989422804014327


def kernel(
    dims,
    inputs, cotangent, gains, biases, w_qkv, w_out, w_router, w_in, w_up, routes,
    o_outs, o_grads, o_gain, o_bias, o_qkv, o_attn, o_router, o_in, o_up,
    xin, cot, rt, gn, bs, wq, wo, wr, wi, wu,
    place, bias, heads_mask, s0, s1, m0, m1, wr128,
    states, norm1, packed, probs, blended, attended, norm2, shares,
    pick0, pick1, stage_out, stage_grad,
    snd, rcv, rows_in, hidden, slope, acc, gbuf, gblend, gpacked, small,
    part, part_in, part_acc, part_dp,
    dense, dense_in, dense_acc, dense_dp, dense_out, dense_last,
    in_sem, w_send, w_recv, e_send, e_recv, f_send,
    a_send, a_recv, a_loc, o_send, o_recv, o_loc,
    g_send, g_recv, gd_send, gd_recv, d_send, d_recv, dx_send, dx_recv, dy_send, dy_recv, fin_sem,
):
    sections, experts, dps, tokens, features, cap, ffs, micro = dims
    images = tokens // SEQ
    total = images * ROWS
    slots = experts * cap
    half = features // 2
    pairs = HEADS // 2
    span = 2 * HEAD_DIM
    rows_dp = features // dps
    rows_own = rows_dp // experts
    width = dense.shape[-1]

    s = lax.axis_index("section")
    e = lax.axis_index("expert")
    d = lax.axis_index("dp")
    twin = (1 - s, e, d)

    def expert_peer(j):
        return (s, lax.rem(e + j, experts), d)

    def dp_peer(j):
        return (s, e, lax.rem(d + j, dps))

    def remote(src, dst, send, recv, device):
        return pltpu.make_async_remote_copy(
            src_ref=src, dst_ref=dst, send_sem=send, recv_sem=recv,
            device_id=device, device_id_type=MESH,
        )

    def arrived(ref, sem):
        pltpu.make_async_copy(ref, ref, sem).wait()

    def each(low, high, body):
        def step(j, carry):
            body(j)
            return carry
        lax.fori_loop(low, high, step, 0)

    barrier = pltpu.get_barrier_semaphore()
    each(1, experts, lambda j: pl.semaphore_signal(
        barrier, inc=1, device_id=expert_peer(j), device_id_type=MESH))
    each(1, dps, lambda j: pl.semaphore_signal(
        barrier, inc=1, device_id=dp_peer(j), device_id_type=MESH))
    pl.semaphore_signal(barrier, inc=1, device_id=twin, device_id_type=MESH)

    load_x = pltpu.make_async_copy(inputs.at[s], xin, in_sem.at[0])
    load_c = pltpu.make_async_copy(cotangent.at[s], cot, in_sem.at[1])
    load_x.start()
    dense_args = (
        (w_qkv, wq), (w_out, wo), (w_router, wr), (gains, gn), (biases, bs),
    )
    for i, (arg, kept) in enumerate(dense_args):
        pltpu.make_async_copy(arg.at[0], kept.at[s], w_recv.at[s, i]).start()
    pltpu.make_async_copy(routes.at[0, s], rt.at[s], w_recv.at[s, 5]).start()
    expert_args = ((w_in, wi), (w_up, wu))
    for i, (arg, kept) in enumerate(expert_args):
        pltpu.make_async_copy(arg.at[0, 0], kept.at[s, d], e_recv.at[i, s, d]).start()
    load_c.start()

    row = iota((total, tokens), 0)
    place[...] = jnp.where(
        ((row & (ROWS - 1)) < SEQ)
        & (iota((total, tokens), 1) == (row >> 6) * SEQ + (row & (ROWS - 1))),
        1.0, 0.0,
    ).astype(BF16)
    query = iota((total, total), 0)
    key = iota((total, total), 1)
    bias[...] = jnp.where(
        ((query >> 6) == (key >> 6)) & ((key & (ROWS - 1)) < SEQ), 0.0, -1e30
    )
    heads_mask[...] = jnp.where(iota((total, span), 1) < HEAD_DIM, 1.0, 0.0).astype(BF16)
    load_x.wait()
    states[0] = nn(place[...], xin[...]).astype(BF16)

    pl.semaphore_wait(barrier, experts - 1 + dps - 1 + 1)

    def dense_copy(i):
        arg, kept = dense_args[i]
        return remote(arg.at[0], kept.at[s], w_send.at[i], w_recv.at[s, i], twin)

    def route_copy():
        return remote(routes.at[0, 1 - s], rt.at[s], w_send.at[5], w_recv.at[s, 5], twin)

    def expert_twin(i):
        arg, kept = expert_args[i]
        return remote(arg.at[0, 0], kept.at[s, d], e_send.at[i, 0], e_recv.at[i, s, d], twin)

    def expert_dp(i, j):
        arg, kept = expert_args[i]
        return remote(arg.at[0, 0], kept.at[s, d], e_send.at[i, j], e_recv.at[i, s, d], dp_peer(j))

    def expert_forward(i, j):
        kept = expert_args[i][1]
        other = lax.rem(d + j, dps)
        return remote(
            kept.at[s, other], kept.at[s, other], f_send.at[i, j], e_recv.at[i, s, other], twin
        )

    def spread_experts():
        for i in range(2):
            each(1, dps, lambda j, i=i: expert_dp(i, j).start())

    for i in (3, 4, 0, 1, 2):
        dense_copy(i).start()
    route_copy().start()

    @pl.when(s == 0)
    def _():
        spread_experts()

    for i in range(2):
        expert_twin(i).start()

    def route(l):
        arrived(rt.at[l], w_recv.at[l, 5])
        named = nn(place[...], rt[l].astype(F32).astype(BF16))
        lane2 = iota((total, 2), 1)
        first = jnp.sum(jnp.where(lane2 == 0, named, 0.0), axis=1, keepdims=True)
        second = jnp.sum(jnp.where(lane2 == 1, named, 0.0), axis=1, keepdims=True)
        live = (iota((total, 1), 0) & (ROWS - 1)) < SEQ
        lane = iota((total, EXTRA), 1).astype(F32)
        hit0 = jnp.where(lane == jnp.where(live, first, -1.0), 1.0, 0.0)
        hit1 = jnp.where(lane == jnp.where(live, second, -1.0), 1.0, 0.0)
        below = jnp.where(iota((total, total), 1) < iota((total, total), 0), 1.0, 0.0).astype(BF16)
        before0 = nn(below, hit0.astype(BF16))
        before1 = nn(below, hit1.astype(BF16)) + jnp.sum(hit0, axis=0, keepdims=True)
        slot0 = first * cap + jnp.sum(hit0 * before0, axis=1, keepdims=True)
        slot1 = second * cap + jnp.sum(hit1 * before1, axis=1, keepdims=True)
        place_of = iota((total, slots), 1).astype(F32)
        s0[l] = jnp.where(place_of == jnp.where(live, slot0, -1.0), 1.0, 0.0).astype(BF16)
        s1[l] = jnp.where(place_of == jnp.where(live, slot1, -1.0), 1.0, 0.0).astype(BF16)
        m0[l] = hit0
        m1[l] = hit1

    each(0, 2, route)

    def exchange_send(phase, values):
        blocks = values.reshape(experts, cap, features)
        snd[...] = jnp.concatenate([blocks[:, :, :half], blocks[:, :, half:]], axis=1).astype(BF16)

        def start(j):
            peer = expert_peer(j)
            remote(
                snd.at[peer[1]], rcv.at[phase, e], a_send.at[j], a_recv.at[phase, j], peer
            ).start()
        each(1, experts, start)
        pltpu.make_async_copy(snd.at[e], rcv.at[phase, e], a_loc).start()

    def exchange_recv(phase):
        def finish(j):
            peer = expert_peer(j)
            source = lax.rem(e - j + experts, experts)
            copy = remote(
                snd.at[peer[1]], rcv.at[phase, source], a_send.at[j], a_recv.at[phase, j], peer
            )
            copy.wait_send()
            copy.wait_recv()
        each(1, experts, finish)
        pltpu.make_async_copy(snd.at[e], rcv.at[phase, e], a_loc).wait()
        blocks = rcv[phase].astype(F32)
        blocks = jnp.concatenate([blocks[:, :cap], blocks[:, cap:]], axis=2)
        return blocks.reshape(slots, features).astype(BF16)

    def gate_parts(l):
        p = shares[l]
        hit0, hit1 = m0[l], m1[l]
        live = (iota((total, 1), 0) & (ROWS - 1)) < SEQ
        pair = jnp.sum(p * (hit0 + hit1), axis=1, keepdims=True)
        inverse = 1.0 / jnp.where(live, pair, 1.0)
        gate0 = jnp.sum(p * hit0, axis=1, keepdims=True) * inverse
        gate1 = jnp.sum(p * hit1, axis=1, keepdims=True) * inverse
        return p, hit0, hit1, inverse, gate0, gate1

    def out_copy(kind, l, stage, dest):
        return remote(stage.at[l], dest.at[0, s], o_send.at[kind], o_recv.at[kind], twin)

    def out_keep(kind, l, stage, dest):
        return pltpu.make_async_copy(stage.at[l], dest.at[0, s], o_loc.at[kind])

    def hand_out(kind, l, stage, dest):
        @pl.when(s == l)
        def _():
            out_keep(kind, l, stage, dest).start()

        @pl.when(s != l)
        def _():
            out_copy(kind, l, stage, dest).start()

    def forward(l):
        for i, (_, kept) in enumerate(dense_args):
            arrived(kept.at[l], w_recv.at[l, i])
        spread = jnp.where(iota((experts, EXTRA), 0) == iota((experts, EXTRA), 1), 1.0, 0.0)
        wr128[l] = nn(wr[l], spread.astype(BF16)).astype(BF16)
        current = states[l].astype(F32)
        norm, _ = normalized(current)
        normed = (norm * gn[l, 0:1] + bs[l, 0:1]).astype(BF16)
        norm1[l] = normed
        packed[l] = nn(normed, wq[l]).astype(BF16)

        def attend(p):
            at = pl.multiple_of(p * span, span)
            queries = packed[l, :, pl.ds(at, span)]
            keys = packed[l, :, pl.ds(features + at, span)]
            values = packed[l, :, pl.ds(2 * features + at, span)]
            left = heads_mask[...]
            found = []
            for h in range(2):
                mask = left if h == 0 else (1.0 - left.astype(F32)).astype(BF16)
                scores = nt(queries * mask, keys) * HEAD_DIM ** (-0.5) + bias[...]
                scores = jnp.exp(scores - jnp.max(scores, axis=-1, keepdims=True))
                prob = scores * (1.0 / jnp.sum(scores, axis=-1, keepdims=True))
                probs[l, 2 * p + h] = prob
                found.append(nn(prob.astype(BF16), values))
            blended[l, :, pl.ds(at, span)] = jnp.where(
                iota((total, span), 1) < HEAD_DIM, found[0], found[1]
            ).astype(BF16)

        each(0, pairs, attend)
        middle = current + nn(blended[l], wo[l])
        attended[l] = middle
        norm, _ = normalized(middle)
        normed = (norm * gn[l, 1:2] + bs[l, 1:2]).astype(BF16)
        norm2[l] = normed
        exchange_send(4 * l, tn(s0[l] + s1[l], normed))

        logits = nn(normed, wr128[l])
        logits = jnp.where(iota((total, EXTRA), 1) < experts, logits, -1e30)
        logits = jnp.exp(logits - jnp.max(logits, axis=-1, keepdims=True))
        shares[l] = logits * (1.0 / jnp.sum(logits, axis=-1, keepdims=True))

        @pl.when(s == l)
        def _():
            for i, (_, kept) in enumerate(expert_args):
                arrived(kept.at[l, d], e_recv.at[i, l, d])

            def pass_on(j):
                other = lax.rem(d + j, dps)
                for i, (_, kept) in enumerate(expert_args):
                    arrived(kept.at[l, other], e_recv.at[i, l, other])
                    expert_forward(i, j).start()
            each(1, dps, pass_on)

        rows = exchange_recv(4 * l)
        rows_in[l] = rows

        @pl.when(s != l)
        def _():
            def get(j):
                for i, (_, kept) in enumerate(expert_args):
                    arrived(kept.at[l, j], e_recv.at[i, l, j])
            each(0, dps, get)

        @pl.when((s == 1) & (l == 0))
        def _():
            spread_experts()

        acc[...] = jnp.zeros_like(acc)

        def expert(b):
            after, dslope = gelu_parts(nn(rows_in[l], wi[l, b]))
            after = after.astype(BF16)
            hidden[l, b] = after
            slope[l, b] = dslope.astype(BF16)
            acc[...] += nn(after, wu[l, b])
        each(0, dps, expert)
        exchange_send(4 * l + 1, acc[...])
        _, _, _, _, gate0, gate1 = gate_parts(l)
        back = exchange_recv(4 * l + 1)
        picked0 = nn(s0[l], back)
        picked1 = nn(s1[l], back)
        pick0[l] = picked0.astype(BF16)
        pick1[l] = picked1.astype(BF16)
        result = (attended[l] + gate0 * picked0 + gate1 * picked1).astype(BF16)
        states[l + 1] = result
        stage_out[l] = tn(place[...], result).astype(BF16)
        hand_out(0, l, stage_out, o_outs)

    each(0, 2, forward)

    load_c.wait()
    gbuf[...] = nn(place[...], cot[...]).astype(BF16)

    def part_copy(b, k):
        return remote(part.at[b, k], part_in.at[b, k], g_send.at[b, k], g_recv.at[b, k], twin)

    def part_dp_copy(j, k):
        other = lax.rem(d + j, dps)
        return remote(
            part.at[other, k], part_dp.at[j - 1, k], gd_send.at[j, k], gd_recv.at[j, k], dp_peer(j)
        )

    def dense_twin():
        return remote(dense, dense_in, d_send, d_recv, twin)

    def dense_dp_copy(j):
        other = lax.rem(d + j, dps)
        return remote(
            dense.at[other], dense_dp.at[j - 1], dx_send.at[j], dx_recv.at[j], dp_peer(j)
        )

    def dense_pair():
        arrived(dense_in, d_recv)

        def pair_sum(j):
            other = lax.rem(d + j, dps)
            dense[other] = (dense[other].astype(F32) + dense_in[other].astype(F32)).astype(BF16)
            dense_dp_copy(j).start()
        each(1, dps, pair_sum)
        dense_acc[...] = dense[d].astype(F32) + dense_in[d].astype(F32)

    def last_copy(j, place_at):
        peer = expert_peer(j)
        return remote(
            dense_out.at[peer[1]], dense_last.at[place_at], dy_send.at[j], dy_recv.at[j], peer
        )

    def dense_dp_sum():
        def dp_sum(j):
            copy = dense_dp_copy(j)
            copy.wait_send()
            copy.wait_recv()
            dense_acc[...] += dense_dp[j - 1].astype(F32)
        each(1, dps, dp_sum)
        blocks = dense_acc[...].reshape(experts, rows_own, width)
        dense_out[...] = jnp.concatenate(
            [blocks[:, :, : width // 2], blocks[:, :, width // 2:]], axis=1
        ).astype(BF16)
        each(1, experts, lambda j: last_copy(j, e).start())

    def backward(step):
        l = 1 - step
        grad_y = gbuf[...].astype(F32)
        p, hit0, hit1, inverse, gate0, gate1 = gate_parts(l)
        exchange_send(
            4 * l + 2,
            tn(s0[l], (gate0 * grad_y).astype(BF16)) + tn(s1[l], (gate1 * grad_y).astype(BF16)),
        )
        gg0 = jnp.sum(grad_y * pick0[l].astype(F32), axis=1, keepdims=True)
        gg1 = jnp.sum(grad_y * pick1[l].astype(F32), axis=1, keepdims=True)
        mixed = gate0 * gg0 + gate1 * gg1
        q = (hit0 * (gg0 - mixed) + hit1 * (gg1 - mixed)) * inverse
        glog = p * (q - jnp.sum(p * q, axis=1, keepdims=True))
        glog_high, glog_low = split_sum(glog)
        extra = tn(norm2[l], glog_high) + tn(norm2[l], glog_low)
        from_gate = nt(glog_high, wr128[l]) + nt(glog_low, wr128[l])

        @pl.when((s == 0) & (l == 0))
        def _():
            def done(b):
                for k in range(2):
                    part_copy(b, k).wait_send()
            each(0, dps, done)

        @pl.when((s == 1) & (l == 0))
        def _():
            def done(j):
                for k in range(2):
                    part_dp_copy(j, k).wait_send()
            each(1, dps, done)

            dense_pair()

        grads = exchange_recv(4 * l + 2)
        acc[...] = jnp.zeros_like(acc)
        snd_rows = grads

        def expert(b):
            before = (nt(snd_rows, wu[l, b]) * slope[l, b].astype(F32)).astype(BF16)
            slope[l, b] = before
            acc[...] += nt(before, wi[l, b])
        each(0, dps, expert)
        exchange_send(4 * l + 3, acc[...])

        def weights(b):
            part[b, 0] = tn(rows_in[l], slope[l, b]).astype(BF16)
            part[b, 1] = tn(hidden[l, b], snd_rows).astype(BF16)

            @pl.when(s != l)
            def _():
                for k in range(2):
                    part_copy(b, k).start()
        each(0, dps, weights)

        @pl.when((s == 1) & (l == 0))
        def _():
            dense_dp_sum()

        @pl.when((s == 0) & (l == 0))
        def _():
            dense_twin().wait_send()

        back = exchange_recv(4 * l + 3)
        grad_normed = nn(s0[l] + s1[l], back) + from_gate
        norm, root = normalized(attended[l])
        small[0:1] = jnp.sum(grad_normed * norm, axis=0, keepdims=True)
        small[1:2] = jnp.sum(grad_normed, axis=0, keepdims=True)
        grad_att = grad_y + norm_back(grad_normed, norm, root, gn[l, 1:2])

        @pl.when(s == l)
        def _():
            for k in range(2):
                arrived(part_in.at[d, k], g_recv.at[d, k])
                part_acc[k] = part[d, k].astype(F32) + part_in[d, k].astype(F32)

            def add(j):
                other = lax.rem(d + j, dps)
                for k in range(2):
                    arrived(part_in.at[other, k], g_recv.at[other, k])
                    part[other, k] = (
                        part[other, k].astype(F32) + part_in[other, k].astype(F32)
                    ).astype(BF16)
                    part_dp_copy(j, k).start()
            each(1, dps, add)

        branch = grad_att.astype(BF16)
        gblend[...] = nt(branch, wo[l]).astype(BF16)

        def put(values, at):
            size = values.shape[1]
            blocks = values.reshape(experts, dps, rows_own, size)
            for b in range(dps):
                dense[b, :, pl.ds(at, size)] = (
                    blocks[:, b].reshape(rows_dp, size).astype(BF16)
                )

        put(tn(blended[l], branch), 3 * features)

        def attend(p):
            at = pl.multiple_of(p * span, span)
            queries = packed[l, :, pl.ds(at, span)]
            keys = packed[l, :, pl.ds(features + at, span)]
            values = packed[l, :, pl.ds(2 * features + at, span)]
            grad_out = gblend[:, pl.ds(at, span)]
            left = heads_mask[...]
            found = []
            for h in range(2):
                mask = left if h == 0 else (1.0 - left.astype(F32)).astype(BF16)
                prob = probs[l, 2 * p + h]
                grad_prob = nt(grad_out * mask, values)
                grad_value = tn(prob.astype(BF16), grad_out)
                grad_score = prob * (
                    grad_prob - jnp.sum(prob * grad_prob, axis=-1, keepdims=True)
                )
                grad_score = grad_score.astype(BF16)
                found.append((
                    nn(grad_score, keys) * HEAD_DIM ** (-0.5),
                    tn(grad_score, queries) * HEAD_DIM ** (-0.5),
                    grad_value,
                ))
            for i in range(3):
                gpacked[:, pl.ds(i * features + at, span)] = jnp.where(
                    iota((total, span), 1) < HEAD_DIM, found[0][i], found[1][i]
                ).astype(BF16)

        each(0, pairs, attend)
        grad_normed = nt(gpacked[...], wq[l])
        current = states[l].astype(F32)
        norm, root = normalized(current)
        small[2:3] = jnp.sum(grad_normed * norm, axis=0, keepdims=True)
        small[3:4] = jnp.sum(grad_normed, axis=0, keepdims=True)
        result = (grad_att + norm_back(grad_normed, norm, root, gn[l, 0:1])).astype(BF16)
        gbuf[...] = result
        stage_grad[l] = tn(place[...], result).astype(BF16)
        hand_out(1, l, stage_grad, o_grads)
        for i in range(3):
            put(tn(norm1[l], gpacked[:, i * features:(i + 1) * features]), i * features)
        high, low = split_sum(small[...])
        lane = iota((8, EXTRA), 1)
        line = iota((8, EXTRA), 0)
        column = jnp.where((lane == line + experts) & (line < 4), 1.0, 0.0).astype(BF16)
        put(extra + tn(high, column) + tn(low, column), 4 * features)

        @pl.when(s != l)
        def _():
            dense_twin().start()

    small[...] = jnp.zeros_like(small)
    dense[:, :, pl.ds(4 * features + EXTRA, width - 4 * features - EXTRA)] = jnp.zeros(
        (dps, rows_dp, width - 4 * features - EXTRA), BF16
    )
    each(0, 2, backward)

    @pl.when(s == 0)
    def _():
        dense_pair()
        dense_dp_sum()

    def part_sum(j):
        for k in range(2):
            arrived(part_dp.at[j - 1, k], gd_recv.at[j, k])
            part_acc[k] += part_dp[j - 1, k].astype(F32)
    each(1, dps, part_sum)
    keep_in = pltpu.make_async_copy(part_acc.at[0], o_in.at[0, 0], fin_sem.at[0])
    keep_up = pltpu.make_async_copy(part_acc.at[1], o_up.at[0, 0], fin_sem.at[1])
    keep_in.start()
    keep_up.start()

    dense_last[e] = dense_out[e]

    def last_wait(j):
        copy = last_copy(j, lax.rem(e - j + experts, experts))
        copy.wait_send()
        copy.wait_recv()
    each(1, experts, last_wait)
    final = jnp.sum(dense_last[...].astype(F32), axis=0)
    final = jnp.concatenate([final[:rows_own], final[rows_own:]], axis=1)
    o_qkv[0] = final[:, : 3 * features]
    o_attn[0] = final[:, 3 * features: 4 * features]
    tail = final[:, 4 * features: 4 * features + EXTRA]
    o_router[0] = tail[:, :experts]
    tail_high, tail_low = split_sum(tail)
    tail_low, tail_rest = split_sum(tail - tail_high.astype(F32))

    def column_rows(late, early):
        lane = iota((2, EXTRA), 1)
        line = iota((2, EXTRA), 0)
        wanted = jnp.where(line == 0, experts + early, experts + late)
        pick = jnp.where(lane == wanted, 1.0, 0.0).astype(BF16)
        return nt(pick, tail_high) + nt(pick, tail_low) + nt(pick, tail_rest)

    o_gain[0] = column_rows(0, 2)
    o_bias[0] = column_rows(1, 3)

    for i in range(5):
        dense_copy(i).wait_send()
    route_copy().wait_send()
    for i in range(2):
        expert_twin(i).wait_send()

        def spread_done(j, i=i):
            expert_dp(i, j).wait_send()
            expert_forward(i, j).wait_send()
        each(1, dps, spread_done)

    @pl.when(s == 0)
    def _():
        def done(j):
            for k in range(2):
                part_dp_copy(j, k).wait_send()
        each(1, dps, done)

    @pl.when(s == 1)
    def _():
        def done(b):
            for k in range(2):
                part_copy(b, k).wait_send()
        each(0, dps, done)
        dense_twin().wait_send()

    for kind, stage, dest in ((0, stage_out, o_outs), (1, stage_grad, o_grads)):
        out_copy(kind, 1 - s, stage, dest).wait_send()
        arrived(dest.at[0, 1 - s], o_recv.at[kind])
        out_keep(kind, s, stage, dest).wait()
    keep_in.wait()
    keep_up.wait()


def local(dims, *args):
    sections, experts, dps, tokens, features, cap, ffs, micro = dims
    total = tokens // SEQ * ROWS
    slots = experts * cap
    rows_dp = features // dps
    rows_own = rows_dp // experts
    width = -(-(4 * features + EXTRA) // 256) * 256
    half = features // 2
    block = ffs // dps
    dma = pltpu.SemaphoreType.DMA
    anywhere = pl.BlockSpec(memory_space=pl.ANY)
    vmem = pl.BlockSpec(memory_space=pltpu.VMEM)

    def out(*shape, dtype=F32):
        return jax.ShapeDtypeStruct(shape, dtype)

    out_shape = (
        out(1, micro, tokens, features, dtype=BF16),
        out(1, micro, tokens, features, dtype=BF16),
        out(1, 2, rows_own),
        out(1, 2, rows_own),
        out(1, rows_own, 3 * features),
        out(1, rows_own, features),
        out(1, rows_own, experts),
        out(1, 1, features, block),
        out(1, 1, block, features),
    )
    V = pltpu.VMEM
    scratch = [
        V((tokens, features), BF16), V((tokens, features), BF16), V((2, tokens, 2), jnp.int32),
        V((2, 2, features), F32), V((2, 2, features), F32),
        V((2, features, 3 * features), BF16), V((2, features, features), BF16),
        V((2, features, experts), BF16),
        V((2, dps, features, block), BF16), V((2, dps, block, features), BF16),
        V((total, tokens), BF16), V((total, total), F32), V((total, 2 * HEAD_DIM), BF16),
        V((2, total, slots), BF16), V((2, total, slots), BF16),
        V((2, total, EXTRA), F32), V((2, total, EXTRA), F32), V((2, features, EXTRA), BF16),
        V((3, total, features), BF16), V((2, total, features), BF16),
        V((2, total, 3 * features), BF16), V((2, HEADS, total, total), F32),
        V((2, total, features), BF16), V((2, total, features), F32),
        V((2, total, features), BF16), V((2, total, EXTRA), F32),
        V((2, total, features), BF16), V((2, total, features), BF16),
        V((2, tokens, features), BF16), V((2, tokens, features), BF16),
        V((experts, 2 * cap, half), BF16), V((8, experts, 2 * cap, half), BF16),
        V((2, slots, features), BF16),
        V((2, dps, slots, block), BF16), V((2, dps, slots, block), BF16),
        V((slots, features), F32),
        V((total, features), BF16), V((total, features), BF16), V((total, 3 * features), BF16),
        V((8, features), F32),
        V((dps, 2, features, block), BF16), V((dps, 2, features, block), BF16),
        V((2, features, block), F32), V((dps - 1, 2, features, block), BF16),
        V((dps, rows_dp, width), BF16), V((dps, rows_dp, width), BF16),
        V((rows_dp, width), F32), V((dps - 1, rows_dp, width), BF16),
        V((experts, 2 * rows_own, width // 2), BF16), V((experts, 2 * rows_own, width // 2), BF16),
        dma((2,)), dma((6,)), dma((2, 6)), dma((2, dps)), dma((2, 2, dps)), dma((2, dps)),
        dma((experts,)), dma((8, experts)), dma, dma((2,)), dma((2,)), dma((2,)),
        dma((dps, 2)), dma((dps, 2)), dma((dps, 2)), dma((dps, 2)),
        dma, dma, dma((dps,)), dma((dps,)), dma((experts,)), dma((experts,)), dma((2,)),
    ]
    return pl.pallas_call(
        partial(kernel, dims),
        out_shape=out_shape,
        in_specs=[anywhere, anywhere, vmem, vmem, anywhere, anywhere, vmem, anywhere, anywhere, vmem],
        out_specs=(anywhere, anywhere, vmem, vmem, vmem, vmem, vmem, anywhere, anywhere),
        scratch_shapes=scratch,
        compiler_params=pltpu.CompilerParams(
            collective_id=0, has_side_effects=True, vmem_limit_bytes=62 * 2**20
        ),
        cost_estimate=pl.CostEstimate(
            flops=10_000_000_000, bytes_accessed=10_000_000, transcendentals=4_000_000
        ),
    )(*args)


def solution(mesh):
    sections, experts, dps = (mesh.shape[name] for name in ("section", "expert", "dp"))

    def run(*args):
        tokens, features = args[0].shape[1:]
        micro = args[0].shape[0]
        cap = 5 * tokens // (2 * experts) + 1
        ffs = args[7].shape[3] * dps
        dims = (sections, experts, dps, tokens, features, cap, ffs, micro)
        return local(dims, *args)

    return jax.shard_map(
        run,
        mesh=mesh,
        in_specs=(
            P(None, ("expert", "dp"), None),
            P(None, ("expert", "dp"), None),
            P("section", None, None),
            P("section", None, None),
            P("section", None, None),
            P("section", None, None),
            P("section", None, None),
            P("section", "expert", None, "dp"),
            P("section", "expert", "dp", None),
            P("section", None, ("expert", "dp"), None),
        ),
        out_specs=(
            P("section", None, ("expert", "dp"), None),
            P("section", None, ("expert", "dp"), None),
            P("section", None, ("expert", "dp")),
            P("section", None, ("expert", "dp")),
            P("section", ("expert", "dp"), None),
            P("section", ("expert", "dp"), None),
            P("section", ("expert", "dp"), None),
            P("section", "expert", None, "dp"),
            P("section", "expert", "dp", None),
        ),
        check_vma=False,
    )
```

```python
from functools import partial

import jax
import jax.numpy as jnp
from jax import lax
from jax.experimental import pallas as pl
from jax.experimental.pallas import tpu as pltpu
from jax.sharding import PartitionSpec as P

HEADS = 8
HEAD_DIM = 64
SEQ = 50
ROWS = 64
EPSILON = 1e-06
MESH = pl.DeviceIdType.MESH
F32 = jnp.float32
BF16 = jnp.bfloat16
EXTRA = 128
SIDE = 4
HOPS = (0, 1, 2, 1)
OFFSETS = sorted(
    ((y, z) for y in range(SIDE) for z in range(SIDE) if y or z),
    key=lambda at: -HOPS[at[0]] - HOPS[at[1]],
)


def nn(a, b):
    return lax.dot_general(a, b, (((1,), (0,)), ((), ())), preferred_element_type=F32)


def nt(a, b):
    return lax.dot_general(a, b, (((1,), (1,)), ((), ())), preferred_element_type=F32)


def tn(a, b):
    return lax.dot_general(a, b, (((0,), (0,)), ((), ())), preferred_element_type=F32)


def iota(shape, dim):
    return lax.broadcasted_iota(jnp.int32, shape, dim)


def split_sum(values):
    high = values.astype(BF16)
    return high, (values - high.astype(F32)).astype(BF16)


def normalized(values):
    center = values - jnp.mean(values, axis=-1, keepdims=True)
    root = lax.rsqrt(jnp.mean(center * center, axis=-1, keepdims=True) + EPSILON)
    return center * root, root


def norm_back(grad, norm, root, gain):
    scaled = grad * gain
    return root * (
        scaled
        - jnp.mean(scaled, axis=-1, keepdims=True)
        - norm * jnp.mean(scaled * norm, axis=-1, keepdims=True)
    )


def gelu_parts(x):
    z = jnp.abs(x) * 0.7071067811865476
    t = 1.0 / (1.0 + 0.3275911 * z)
    poly = t * (
        0.254829592 + t * (-0.284496736 + t * (1.421413741 + t * (-1.453152027 + t * 1.061405429)))
    )
    bell = jnp.exp(-z * z)
    tail = 0.5 * poly * bell
    share = jnp.where(x >= 0.0, 1.0 - tail, tail)
    return x * share, share + x * bell * 0.3989422804014327


def kernel(
    dims,
    inputs, cotangent, gains, biases, w_qkv, w_out, w_router, w_in, w_up, routes,
    o_outs, o_grads, o_norms, o_dense, o_in, o_up,
    xin, cot, rt, gn, bs, wq, wo, wr, wi, wu,
    place, s0, s1, m0, m1, wr128,
    states, norm1, packed, probs, blended, attended, norm2, shares,
    pick0, pick1, stage_out, stage_grad, join_out, join_grad,
    snd, rcv, rows_in, hidden, slope, acc, grows, gbuf, branch_kept, gblend, gpacked, small, extra_kept,
    part, part_in, part_acc, ring, ring_end,
    dense, dense_in, dense_acc, dense_dp, dense_out, dense_last,
    second, second_in, second_far, second_out, second_last,
    in_sem, w_send, w_recv, e_send, e_recv, r_send, f_send, t_send,
    a_send, a_recv, o_send, o_recv, o_loc,
    g_send, g_recv, h_send, h_recv, k_send, k_recv,
    d_send, d_recv, dx_send, dx_recv, dy_send, dy_recv, sy_send, sy_recv, sx_send, sx_recv, fin_sem,
):
    sections, experts, dps, tokens, features, cap, ffs, micro = dims
    images = tokens // SEQ
    total = images * ROWS
    slots = experts * cap
    half = features // 2
    pairs = HEADS // 2
    span = 2 * HEAD_DIM
    rows_dp = features // dps
    rows_own = rows_dp // experts
    first_width = dense.shape[-1]
    second_width = second.shape[-1]
    scale = HEAD_DIM ** (-0.5)

    s = lax.axis_index("section")
    e = lax.axis_index("expert")
    d = lax.axis_index("dp")
    e_y, e_z = e // SIDE, lax.rem(e, SIDE)
    twin = (1 - s, e, d)

    def expert_at(y, z, sign=1):
        return (
            lax.rem(e_y + SIDE + sign * y, SIDE) * SIDE + lax.rem(e_z + SIDE + sign * z, SIDE)
        )

    def around(j):
        return lax.rem(d + j, dps)

    right, left, far = around(1), around(3), around(2)
    to_right, to_left, to_far = (s, e, right), (s, e, left), (s, e, far)

    def remote(src, dst, send, recv, device):
        return pltpu.make_async_remote_copy(
            src_ref=src, dst_ref=dst, send_sem=send, recv_sem=recv,
            device_id=device, device_id_type=MESH,
        )

    def arrived(ref, sem):
        pltpu.make_async_copy(ref, ref, sem).wait()

    def each(low, high, body):
        def step(j, carry):
            body(j)
            return carry
        lax.fori_loop(low, high, step, 0)

    barrier = pltpu.get_barrier_semaphore()
    pl.semaphore_signal(barrier, inc=1, device_id=twin, device_id_type=MESH)
    for device in (to_right, to_left, to_far):
        pl.semaphore_signal(barrier, inc=1, device_id=device, device_id_type=MESH)
    for y, z in OFFSETS:
        pl.semaphore_signal(
            barrier, inc=1, device_id=(s, expert_at(y, z), d), device_id_type=MESH
        )

    load_x = pltpu.make_async_copy(inputs, xin, in_sem.at[0])
    load_c = pltpu.make_async_copy(cotangent, cot, in_sem.at[1])
    load_x.start()
    dense_args = (
        (w_qkv, wq), (w_out, wo), (w_router, wr), (gains, gn), (biases, bs),
    )
    for i, (arg, kept) in enumerate(dense_args):
        pltpu.make_async_copy(arg.at[0], kept.at[s], w_recv.at[s, i]).start()
    pltpu.make_async_copy(routes.at[0, s], rt.at[s], w_recv.at[s, 5]).start()
    expert_args = ((w_in, wi), (w_up, wu))
    for i, (arg, kept) in enumerate(expert_args):
        pltpu.make_async_copy(arg.at[0, 0], kept.at[s, d], e_recv.at[i, s, d]).start()
    load_c.start()

    row = iota((total, tokens), 0)
    place[...] = jnp.where(
        ((row & (ROWS - 1)) < SEQ)
        & (iota((total, tokens), 1) == (row >> 6) * SEQ + (row & (ROWS - 1))),
        1.0, 0.0,
    ).astype(BF16)

    def own_micro(ref):
        both = ref[...].astype(F32)
        return jnp.where(s == 0, both[:, 0, :], both[:, 1, :]).astype(BF16)

    load_x.wait()
    states[0] = nn(place[...], own_micro(xin)).astype(BF16)
    small[...] = jnp.zeros_like(small)
    spare = first_width + second_width - 4 * features - EXTRA
    second[:, pl.ds(second_width - spare, spare)] = jnp.zeros((features, spare), BF16)

    pl.semaphore_wait(barrier, 1 + 3 + len(OFFSETS))

    def dense_copy(i):
        arg, kept = dense_args[i]
        return remote(arg.at[0], kept.at[s], w_send.at[i], w_recv.at[s, i], twin)

    def route_copy():
        return remote(routes.at[0, 1 - s], rt.at[s], w_send.at[5], w_recv.at[s, 5], twin)

    def expert_twin(i):
        arg, kept = expert_args[i]
        return remote(arg.at[0, 0], kept.at[s, d], t_send.at[i], e_recv.at[i, s, d], twin)

    def expert_next(i, way):
        arg, kept = expert_args[i]
        return remote(
            arg.at[0, 0], kept.at[s, d], e_send.at[i, way], e_recv.at[i, s, d],
            (to_right, to_left)[way],
        )

    def expert_relay(way):
        kept, other = ((wi, left), (wu, right))[way]
        return remote(
            kept.at[s, other], kept.at[s, other], r_send.at[way], e_recv.at[way, s, other],
            (to_right, to_left)[way],
        )

    def expert_forward(i, j):
        kept = expert_args[i][1]
        other = around(j)
        return remote(
            kept.at[s, other], kept.at[s, other], f_send.at[i, j - 1], e_recv.at[i, s, other], twin
        )

    def spread_experts():
        for i, way in ((0, 0), (1, 1), (1, 0), (0, 1)):
            expert_next(i, way).start()

    def relay(l):
        arrived(wi.at[l, left], e_recv.at[0, l, left])
        expert_relay(0).start()
        expert_forward(0, 3).start()
        arrived(wu.at[l, right], e_recv.at[1, l, right])
        expert_relay(1).start()
        expert_forward(1, 1).start()

    def relay_rest(l):
        arrived(wi.at[l, right], e_recv.at[0, l, right])
        expert_forward(0, 1).start()
        arrived(wu.at[l, left], e_recv.at[1, l, left])
        expert_forward(1, 3).start()

    for i in (3, 4, 0, 1, 2):
        dense_copy(i).start()
    route_copy().start()

    @pl.when(s == 0)
    def _():
        spread_experts()

    for i in range(2):
        expert_twin(i).start()

    live = (iota((total, 1), 0) & (ROWS - 1)) < SEQ

    def route(l):
        arrived(rt.at[l], w_recv.at[l, 5])
        named = nt(place[...], rt[l].astype(F32).astype(BF16))
        lane2 = iota((total, 2), 1)
        first = jnp.sum(jnp.where(lane2 == 0, named, 0.0), axis=1, keepdims=True)
        second = jnp.sum(jnp.where(lane2 == 1, named, 0.0), axis=1, keepdims=True)
        lane = iota((total, EXTRA), 1).astype(F32)
        hit0 = jnp.where(lane == jnp.where(live, first, -1.0), 1.0, 0.0)
        hit1 = jnp.where(lane == jnp.where(live, second, -1.0), 1.0, 0.0)
        below = jnp.where(iota((total, total), 1) < iota((total, total), 0), 1.0, 0.0).astype(BF16)
        before0 = nn(below, hit0.astype(BF16))
        before1 = nn(below, hit1.astype(BF16)) + jnp.sum(hit0, axis=0, keepdims=True)
        slot0 = first * cap + jnp.sum(hit0 * before0, axis=1, keepdims=True)
        slot1 = second * cap + jnp.sum(hit1 * before1, axis=1, keepdims=True)
        place_of = iota((total, slots), 1).astype(F32)
        s0[l] = jnp.where(place_of == jnp.where(live, slot0, -1.0), 1.0, 0.0).astype(BF16)
        s1[l] = jnp.where(place_of == jnp.where(live, slot1, -1.0), 1.0, 0.0).astype(BF16)
        m0[l] = hit0
        m1[l] = hit1

    def exchange_send(phase, way, values):
        blocks = values.reshape(experts, cap, features)
        snd[way] = jnp.concatenate(
            [blocks[:, :, :half], blocks[:, :, half:]], axis=1
        ).astype(BF16)
        for y, z in OFFSETS:
            peer = expert_at(y, z)
            remote(
                snd.at[way, peer], rcv.at[phase, e], a_send.at[way], a_recv.at[phase], (s, peer, d)
            ).start()
        pltpu.make_async_copy(snd.at[way, e], rcv.at[phase, e], a_recv.at[phase]).start()

    def exchange_recv(phase, way):
        arrived(rcv.at[phase], a_recv.at[phase])
        sent = snd.at[way, pl.ds(0, experts - 1)]
        arrived(sent, a_send.at[way])
        blocks = rcv[phase].astype(F32)
        blocks = jnp.concatenate([blocks[:, :cap], blocks[:, cap:]], axis=2)
        return blocks.reshape(slots, features).astype(BF16)

    def gate_parts(l):
        p = shares[l]
        hit0, hit1 = m0[l], m1[l]
        pair = jnp.sum(p * (hit0 + hit1), axis=1, keepdims=True)
        inverse = 1.0 / jnp.where(live, pair, 1.0)
        gate0 = jnp.sum(p * hit0, axis=1, keepdims=True) * inverse
        gate1 = jnp.sum(p * hit1, axis=1, keepdims=True) * inverse
        return p, hit0, hit1, inverse, gate0, gate1

    def out_copy(kind, l, stage):
        return remote(
            stage.at[l], (stage_out, stage_grad)[kind].at[2], o_send.at[kind], o_recv.at[kind], twin
        )

    def hand_out(kind, l, stage, values):
        stage[l] = tn(place[...], values).astype(BF16)

        @pl.when(s != l)
        def _():
            out_copy(kind, l, stage).start()

    def join(kind, stage, joined, dest):
        arrived(stage.at[2], o_recv.at[kind])
        own = stage[s].astype(F32)
        other = stage[2].astype(F32)
        joined[...] = jnp.stack(
            [jnp.where(s == 0, own, other), jnp.where(s == 0, other, own)], axis=1
        ).astype(BF16)
        return pltpu.make_async_copy(joined, dest, o_loc.at[kind])

    def pair_keys(ref_rows, side):
        return jnp.concatenate([ref_rows * side, ref_rows * (1.0 - side)], axis=0).astype(BF16)

    lane_side = jnp.where(iota((1, span), 1) < HEAD_DIM, 1.0, 0.0)
    in_left = iota((total, span), 1) < HEAD_DIM

    def attention(l):
        for i, (_, kept) in enumerate(dense_args):
            arrived(kept.at[l], w_recv.at[l, i])
        current = states[l].astype(F32)
        norm, _ = normalized(current)
        normed = (norm * gn[l, 0:1] + bs[l, 0:1]).astype(BF16)
        norm1[l] = normed
        packed[l] = nn(normed, wq[l]).astype(BF16)
        key_bias = jnp.where((iota((1, span), 1) & (ROWS - 1)) < SEQ, 0.0, -1e30)
        for p in range(pairs):
            at = p * span
            scores = jnp.concatenate([
                nt(
                    packed[l, i * ROWS:(i + 1) * ROWS, at:at + span],
                    pair_keys(packed[
                        l, i * ROWS:(i + 1) * ROWS, features + at:features + at + span
                    ].astype(F32), lane_side),
                )
                for i in range(images)
            ], axis=0) * scale + key_bias
            top0 = jnp.max(jnp.where(in_left, scores, -1e30), axis=-1, keepdims=True)
            top1 = jnp.max(jnp.where(in_left, -1e30, scores), axis=-1, keepdims=True)
            powers = jnp.exp(scores - jnp.where(in_left, top0, top1))
            sum0 = jnp.sum(jnp.where(in_left, powers, 0.0), axis=-1, keepdims=True)
            sum1 = jnp.sum(jnp.where(in_left, 0.0, powers), axis=-1, keepdims=True)
            prob = powers * jnp.where(in_left, 1.0 / sum0, 1.0 / sum1)
            probs[l, p] = prob
            low = prob.astype(BF16)
            for i in range(images):
                values = packed[
                    l, i * ROWS:(i + 1) * ROWS, 2 * features + at:2 * features + at + span
                ].astype(F32)
                blended[l, i * ROWS:(i + 1) * ROWS, at:at + span] = nn(
                    low[i * ROWS:(i + 1) * ROWS], pair_keys(values, lane_side)
                ).astype(BF16)
        middle = current + nn(blended[l], wo[l])
        attended[l] = middle
        norm, _ = normalized(middle)
        normed = (norm * gn[l, 1:2] + bs[l, 1:2]).astype(BF16)
        norm2[l] = normed
        exchange_send(4 * l, 0, tn(s0[l] + s1[l], normed))
        spread = jnp.where(iota((EXTRA, experts), 0) == iota((EXTRA, experts), 1), 1.0, 0.0)
        wr128[l] = nn(spread.astype(BF16), wr[l]).astype(BF16)
        logits = nt(normed, wr128[l])
        logits = jnp.where(iota((total, EXTRA), 1) < experts, logits, -1e30)
        logits = jnp.exp(logits - jnp.max(logits, axis=-1, keepdims=True))
        shares[l] = logits * (1.0 / jnp.sum(logits, axis=-1, keepdims=True))

    def block_at(step):
        return around(step + step // 2 - 2 * (step // 3))

    def expert_forward_pass(l):
        rows_in[l] = exchange_recv(4 * l, 0)
        acc[...] = jnp.zeros_like(acc)

        def block(step):
            b = block_at(step)

            @pl.when((s == l) & (step == 0))
            def _():
                for i, (_, kept) in enumerate(expert_args):
                    arrived(kept.at[l, d], e_recv.at[i, l, d])

            @pl.when((s == l) & (step == 3))
            def _():
                for i, (_, kept) in enumerate(expert_args):
                    arrived(kept.at[l, far], e_recv.at[i, l, far])
                    expert_forward(i, 2).start()

            @pl.when(s != l)
            def _():
                for i, (_, kept) in enumerate(expert_args):
                    arrived(kept.at[l, b], e_recv.at[i, l, b])

            after, dslope = gelu_parts(nn(rows_in[l], wi[l, b]))
            after = after.astype(BF16)
            hidden[l, b] = after
            slope[l, b] = dslope.astype(BF16)
            acc[...] += nn(after, wu[l, b])
        each(0, dps, block)
        exchange_send(4 * l + 1, 0, acc[...])

    def slot_grads(l, way, grad_y, gate0, gate1):
        exchange_send(
            4 * l + 2, way,
            tn(s0[l], (gate0 * grad_y).astype(BF16)) + tn(s1[l], (gate1 * grad_y).astype(BF16)),
        )

    def expert_backward_pass(l, way):
        grows[...] = exchange_recv(4 * l + 2, way)
        acc[...] = jnp.zeros_like(acc)

        def block(b):
            before = (nt(grows[...], wu[l, b]) * slope[l, b].astype(F32)).astype(BF16)
            slope[l, b] = before
            acc[...] += nt(before, wi[l, b])
        each(0, dps, block)
        exchange_send(4 * l + 3, way, acc[...])

    def part_copy(b, k):
        return remote(part.at[b, k], part_in.at[b, k], g_send.at[b, k], g_recv.at[b, k], twin)

    def expert_weights(l):
        def block(step):
            b = around(2 + step)
            part[b, 0] = tn(rows_in[l], slope[l, b]).astype(BF16)

            @pl.when(s != l)
            def _():
                part_copy(b, 0).start()

            part[b, 1] = tn(hidden[l, b], grows[...]).astype(BF16)

            @pl.when(s != l)
            def _():
                part_copy(b, 1).start()
        each(0, dps, block)

    def pair_part(b, k):
        arrived(part_in.at[b, k], g_recv.at[b, k])
        return part[b, k].astype(F32) + part_in[b, k].astype(F32)

    def ring_copy(k):
        return remote(
            part.at[far, k], ring.at[k], h_send.at[k], h_recv.at[k], (to_right, to_left)[k]
        )

    def ring_last(way, k):
        return remote(
            part.at[(right, left)[way], k], ring_end.at[way, k], k_send.at[way, k],
            k_recv.at[way, k], (to_right, to_left)[way],
        )

    def ring_first_step():
        for k in range(2):
            part[far, k] = pair_part(far, k).astype(BF16)
            ring_copy(k).start()

    def ring_second_step():
        for way, k in ((0, 1), (1, 0), (0, 0), (1, 1)):
            b = (right, left)[way]
            value = pair_part(b, k)
            if way == k:
                arrived(ring.at[k], h_recv.at[k])
                value = value + ring[k].astype(F32)
            part[b, k] = value.astype(BF16)
            ring_last(way, k).start()
        for k in range(2):
            part_acc[k] = pair_part(d, k)

    def ring_sent():
        for k in range(2):
            ring_copy(k).wait_send()
            for way in range(2):
                ring_last(way, k).wait_send()

    def part_sent():
        def done(b):
            for k in range(2):
                part_copy(b, k).wait_send()
        each(0, dps, done)

    def dense_twin(b):
        return remote(dense.at[b], dense_in.at[b], d_send.at[b], d_recv.at[b], twin)

    def dense_dp_copy(j):
        return remote(
            dense.at[around(j)], dense_dp.at[j - 1], dx_send.at[j - 1], dx_recv.at[j - 1],
            (s, e, around(j)),
        )

    def second_twin():
        return remote(second, second_in, d_send.at[dps], d_recv.at[dps], twin)

    def second_dp_copy(j):
        return remote(
            second_out.at[around(j)], second_last.at[d], sx_send.at[j - 1], sx_recv,
            (s, e, around(j)),
        )

    def narrow(values):
        half_width = values.shape[-1] // 2
        return jnp.concatenate(
            [values[:, :, :half_width], values[:, :, half_width:]], axis=1
        ).astype(BF16)

    def widen(values):
        return jnp.concatenate([values[:rows_own], values[rows_own:]], axis=1)

    def dense_pair():
        arrived(second_in, d_recv.at[dps])
        rows = rows_own * dps

        def pair(j):
            at = pl.ds(pl.multiple_of(j * rows, rows), rows)
            second[at] = (second[at].astype(F32) + second_in[at].astype(F32)).astype(BF16)
        each(0, experts, pair)
        for y, z in OFFSETS:
            peer = expert_at(y, z)
            at = pl.ds(pl.multiple_of(peer * rows, rows), rows)
            remote(second.at[at], second_far.at[e], sy_send, sy_recv, (s, peer, d)).start()
        at = pl.ds(pl.multiple_of(e * rows, rows), rows)
        pltpu.make_async_copy(second.at[at], second_far.at[e], sy_recv).start()
        for j in (2, 1, 3):
            other = around(j)
            arrived(dense_in.at[other], d_recv.at[other])
            dense[other] = (dense[other].astype(F32) + dense_in[other].astype(F32)).astype(BF16)
            dense_dp_copy(j).start()
        arrived(dense_in.at[d], d_recv.at[d])
        dense_acc[...] = dense[d].astype(F32) + dense_in[d].astype(F32)

    def dense_middle():
        arrived(second_far, sy_recv)
        arrived(second.at[pl.ds(0, features - rows_own * dps)], sy_send)
        summed = second_far[0].astype(F32)
        for j in range(1, experts):
            summed = summed + second_far[j].astype(F32)
        second_out[...] = narrow(summed.reshape(dps, rows_own, second_width))
        for j in (2, 1, 3):
            second_dp_copy(j).start()
        pltpu.make_async_copy(second_out.at[d], second_last.at[d], sx_recv).start()
        for j in (1, 3, 2):
            copy = dense_dp_copy(j)
            copy.wait_send()
            copy.wait_recv()
        summed = dense_acc[...]
        for j in range(dps - 1):
            summed = summed + dense_dp[j].astype(F32)
        dense_out[...] = narrow(summed.reshape(experts, rows_own, first_width))
        for y, z in OFFSETS:
            peer = expert_at(y, z)
            remote(
                dense_out.at[peer], dense_last.at[e], dy_send, dy_recv, (s, peer, d)
            ).start()
        pltpu.make_async_copy(dense_out.at[e], dense_last.at[e], dy_recv).start()

    def put(values, at):
        size = values.shape[1]
        if at >= first_width:
            second[:, pl.ds(at - first_width, size)] = values.astype(BF16)
            return
        if at + size > first_width:
            put(values[:, first_width - at:], first_width)
            values = values[:, :first_width - at]
            size = first_width - at
        blocks = values.reshape(experts, dps, rows_own, size)
        for b in range(dps):
            dense[b, :, pl.ds(at, size)] = blocks[:, b].reshape(rows_dp, size).astype(BF16)

    def put_extra(l):
        high, low = split_sum(small[l])
        lane = iota((8, EXTRA), 1)
        line = iota((8, EXTRA), 0)
        column = jnp.where((lane == line + experts) & (line < 4), 1.0, 0.0).astype(BF16)
        put(extra_kept[l] + tn(high, column) + tn(low, column), 4 * features)

    def put_dense(l):
        put(tn(blended[l], branch_kept[...]), 3 * features)
        put_extra(l)
        for i in (2, 1):
            put(tn(norm1[l], gpacked[:, i * features:(i + 1) * features]), i * features)

        @pl.when(s != l)
        def _():
            second_twin().start()

        put(tn(norm1[l], gpacked[:, :features]), 0)

        @pl.when(s != l)
        def _():
            for j in (2, 1, 3, 0):
                dense_twin(around(j)).start()

    def dense_twin_sent():
        second_twin().wait_send()
        for b in range(dps):
            dense_twin(b).wait_send()

    def gate_back(l, grad_y, gates):
        p, hit0, hit1, inverse, gate0, gate1 = gates
        gg0 = jnp.sum(grad_y * pick0[l].astype(F32), axis=1, keepdims=True)
        gg1 = jnp.sum(grad_y * pick1[l].astype(F32), axis=1, keepdims=True)
        mixed = gate0 * gg0 + gate1 * gg1
        q = (hit0 * (gg0 - mixed) + hit1 * (gg1 - mixed)) * inverse
        glog = p * (q - jnp.sum(p * q, axis=1, keepdims=True))
        high, low = split_sum(glog)
        extra_kept[l] = tn(norm2[l], high) + tn(norm2[l], low)
        return nn(high, wr128[l]) + nn(low, wr128[l])

    def attention_back(l, way, grad_y, from_gate, between):
        back = exchange_recv(4 * l + 3, way)
        grad_normed = nn(s0[l] + s1[l], back) + from_gate
        norm, root = normalized(attended[l])
        small[l, 0:1] = jnp.sum(grad_normed * norm, axis=0, keepdims=True)
        small[l, 1:2] = jnp.sum(grad_normed, axis=0, keepdims=True)
        grad_att = grad_y + norm_back(grad_normed, norm, root, gn[l, 1:2])
        branch = grad_att.astype(BF16)
        branch_kept[...] = branch
        gblend[...] = nt(branch, wo[l]).astype(BF16)
        for p in range(pairs):
            at = p * span
            queries = packed[l, :, at:at + span]
            keys = packed[l, :, features + at:features + at + span]
            values = packed[l, :, 2 * features + at:2 * features + at + span]
            prob = probs[l, p]
            low = prob.astype(BF16)
            grad_prob = jnp.concatenate([
                nt(
                    gblend[i * ROWS:(i + 1) * ROWS, at:at + span],
                    pair_keys(values[i * ROWS:(i + 1) * ROWS].astype(F32), lane_side),
                )
                for i in range(images)
            ], axis=0)
            mixed = prob * grad_prob
            sum0 = jnp.sum(jnp.where(in_left, mixed, 0.0), axis=-1, keepdims=True)
            sum1 = jnp.sum(jnp.where(in_left, 0.0, mixed), axis=-1, keepdims=True)
            grad_score = (prob * (grad_prob - jnp.where(in_left, sum0, sum1))).astype(BF16)
            for i in range(images):
                rows = slice(i * ROWS, (i + 1) * ROWS)
                one = grad_score[rows]
                grad_query = nn(one, pair_keys(keys[rows].astype(F32), lane_side)) * scale
                grad_key = tn(one, queries[rows]) * scale
                grad_value = tn(low[rows], gblend[rows, at:at + span])
                side = in_left[:ROWS]
                grad_key = jnp.where(side, grad_key[:ROWS], grad_key[ROWS:])
                grad_value = jnp.where(side, grad_value[:ROWS], grad_value[ROWS:])
                gpacked[rows, at:at + span] = grad_query.astype(BF16)
                gpacked[rows, features + at:features + at + span] = grad_key.astype(BF16)
                gpacked[rows, 2 * features + at:2 * features + at + span] = grad_value.astype(BF16)
        between()
        grad_normed = nt(gpacked[...], wq[l])
        norm, root = normalized(states[l].astype(F32))
        small[l, 2:3] = jnp.sum(grad_normed * norm, axis=0, keepdims=True)
        small[l, 3:4] = jnp.sum(grad_normed, axis=0, keepdims=True)
        return grad_att, grad_normed, norm, root

    def finish_back(l, grad_att, grad_normed, norm, root):
        gbuf[...] = (grad_att + norm_back(grad_normed, norm, root, gn[l, 0:1])).astype(BF16)

    def combine(l, gate0, gate1, way):
        back = exchange_recv(4 * l + 1, way)
        picked0 = nn(s0[l], back)
        picked1 = nn(s1[l], back)
        pick0[l] = picked0.astype(BF16)
        pick1[l] = picked1.astype(BF16)
        states[l + 1] = (attended[l] + gate0 * picked0 + gate1 * picked1).astype(BF16)

    route(0)
    attention(0)

    @pl.when(s == 0)
    def _():
        relay(0)
        relay_rest(0)

    route(1)
    expert_forward_pass(0)

    @pl.when(s == 1)
    def _():
        spread_experts()

    load_c.wait()
    gbuf[...] = nn(place[...], own_micro(cot)).astype(BF16)
    gates = gate_parts(0)
    combine(0, gates[4], gates[5], 0)

    @pl.when(s == 1)
    def _():
        relay(1)

    attention(1)
    gates = gate_parts(1)
    grad_y = gbuf[...].astype(F32)
    slot_grads(1, 1, grad_y, gates[4], gates[5])

    @pl.when(s == 1)
    def _():
        relay_rest(1)

    hand_out(0, 0, stage_out, states[1])
    expert_forward_pass(1)
    expert_backward_pass(1, 1)
    expert_weights(1)
    combine(1, gates[4], gates[5], 0)
    from_gate = gate_back(1, grad_y, gates)

    @pl.when(s == 1)
    def _():
        ring_first_step()

    kept = attention_back(1, 1, grad_y, from_gate, lambda: None)
    finish_back(1, *kept)

    gates = gate_parts(0)
    grad_y = gbuf[...].astype(F32)
    slot_grads(0, 0, grad_y, gates[4], gates[5])
    put_dense(1)

    @pl.when(s == 1)
    def _():
        ring_second_step()

    hand_out(0, 1, stage_out, states[2])
    hand_out(1, 1, stage_grad, gbuf[...])
    from_gate = gate_back(0, grad_y, gates)
    expert_backward_pass(0, 0)

    @pl.when(s == 0)
    def _():
        part_sent()

    @pl.when(s == 1)
    def _():
        ring_sent()

    expert_weights(0)

    @pl.when(s == 0)
    def _():
        ring_first_step()

    @pl.when(s == 1)
    def _():
        dense_pair()

    def between():
        @pl.when(s == 0)
        def _():
            ring_second_step()
            dense_twin_sent()

        @pl.when(s == 1)
        def _():
            dense_middle()

    kept = attention_back(0, 0, grad_y, from_gate, between)
    put_dense(0)
    finish_back(0, *kept)
    hand_out(1, 0, stage_grad, gbuf[...])
    keep_out = join(0, stage_out, join_out, o_outs)
    keep_out.start()

    @pl.when(s == 0)
    def _():
        dense_pair()
        dense_middle()

    for k in range(2):
        for way in range(2):
            arrived(ring_end.at[way, k], k_recv.at[way, k])
            part_acc[k] += ring_end[way, k].astype(F32)
    keep_in = pltpu.make_async_copy(part_acc.at[0], o_in, fin_sem.at[0])
    keep_up = pltpu.make_async_copy(part_acc.at[1], o_up, fin_sem.at[1])
    keep_in.start()
    keep_up.start()
    keep_grad = join(1, stage_grad, join_grad, o_grads)
    keep_grad.start()

    arrived(dense_last, dy_recv)
    arrived(second_last, sx_recv)
    final = jnp.concatenate([
        widen(jnp.sum(dense_last[...].astype(F32), axis=0)),
        widen(jnp.sum(second_last[...].astype(F32), axis=0)),
    ], axis=1)
    o_dense[...] = final
    tail = final[:, 4 * features: 4 * features + EXTRA]
    tail_high, tail_low = split_sum(tail)
    tail_low, tail_rest = split_sum(tail - tail_high.astype(F32))

    def column_rows(late, early):
        lane = iota((2, EXTRA), 1)
        line = iota((2, EXTRA), 0)
        wanted = jnp.where(line == 0, experts + early, experts + late)
        pick = jnp.where(lane == wanted, 1.0, 0.0).astype(BF16)
        return nt(pick, tail_high) + nt(pick, tail_low) + nt(pick, tail_rest)

    o_norms[0] = column_rows(0, 2)
    o_norms[1] = column_rows(1, 3)

    for i in range(5):
        dense_copy(i).wait_send()
    route_copy().wait_send()
    for i in range(2):
        expert_twin(i).wait_send()
        expert_relay(i).wait_send()
        for way in range(2):
            expert_next(i, way).wait_send()
        for j in range(1, dps):
            expert_forward(i, j).wait_send()

    @pl.when(s == 0)
    def _():
        ring_sent()

    @pl.when(s == 1)
    def _():
        part_sent()
        dense_twin_sent()

    out_copy(0, 1 - s, stage_out).wait_send()
    out_copy(1, 1 - s, stage_grad).wait_send()
    arrived(dense_out.at[pl.ds(0, experts - 1)], dy_send)
    for j in range(1, dps):
        second_dp_copy(j).wait_send()
    keep_out.wait()
    keep_grad.wait()
    keep_in.wait()
    keep_up.wait()


def finish(
    features, outs, grads, norms, dense, part_in, part_up,
    o_outs, o_grads, o_gain, o_bias, o_qkv, o_attn, o_router, o_in, o_up,
    v_in, v_up, v_outs, v_grads, sems,
):
    passes = (
        (part_in, v_in, o_in.at[0, 0]), (part_up, v_up, o_up.at[0, 0]),
        (outs, v_outs, o_outs), (grads, v_grads, o_grads),
    )
    loads = [
        pltpu.make_async_copy(source, kept, sems.at[0, i])
        for i, (source, kept, _) in enumerate(passes)
    ]
    copies = [
        pltpu.make_async_copy(kept, dest, sems.at[1, i])
        for i, (_, kept, dest) in enumerate(passes)
    ]
    for load in loads:
        load.start()
    o_gain[0] = norms[0]
    o_bias[0] = norms[1]
    o_qkv[0] = dense[:, : 3 * features]
    o_attn[0] = dense[:, 3 * features: 4 * features]
    o_router[0] = dense[:, 4 * features: 4 * features + o_router.shape[-1]]
    for load, copy in zip(loads, copies):
        load.wait()
        copy.start()
    for copy in copies:
        copy.wait()


def local(
    dims, inputs, cotangent, gains, biases, w_qkv, w_out, w_router, w_in, w_up, routes
):
    sections, experts, dps, tokens, features, cap, ffs, micro = dims
    images = tokens // SEQ
    total = images * ROWS
    slots = experts * cap
    rows_dp = features // dps
    rows_own = rows_dp // experts
    width = -(-(4 * features + EXTRA) // 256) * 256
    first = width // 3
    second = width - first
    half = features // 2
    block = ffs // dps
    dma = pltpu.SemaphoreType.DMA
    anywhere = pl.BlockSpec(memory_space=pl.ANY)
    vmem = pl.BlockSpec(memory_space=pltpu.VMEM)

    def out(*shape, dtype=F32):
        return jax.ShapeDtypeStruct(shape, dtype)

    V = pltpu.VMEM
    pairs, span = HEADS // 2, 2 * HEAD_DIM
    scratch = [
        V((tokens, 2, features), BF16), V((tokens, 2, features), BF16),
        V((2, 2, tokens), jnp.int32),
        V((2, 2, features), F32), V((2, 2, features), F32),
        V((2, features, 3 * features), BF16), V((2, features, features), BF16),
        V((2, experts, features), BF16),
        V((2, dps, features, block), BF16), V((2, dps, block, features), BF16),
        V((total, tokens), BF16),
        V((2, total, slots), BF16), V((2, total, slots), BF16),
        V((2, total, EXTRA), F32), V((2, total, EXTRA), F32), V((2, EXTRA, features), BF16),
        V((3, total, features), BF16), V((2, total, features), BF16),
        V((2, total, 3 * features), BF16), V((2, pairs, total, span), F32),
        V((2, total, features), BF16), V((2, total, features), F32),
        V((2, total, features), BF16), V((2, total, EXTRA), F32),
        V((2, total, features), BF16), V((2, total, features), BF16),
        V((3, tokens, features), BF16), V((3, tokens, features), BF16),
        V((tokens, 2, features), BF16), V((tokens, 2, features), BF16),
        V((2, experts, 2 * cap, half), BF16), V((8, experts, 2 * cap, half), BF16),
        V((2, slots, features), BF16),
        V((2, dps, slots, block), BF16), V((2, dps, slots, block), BF16),
        V((slots, features), F32), V((slots, features), BF16),
        V((total, features), BF16), V((total, features), BF16), V((total, features), BF16),
        V((total, 3 * features), BF16),
        V((2, 8, features), F32), V((2, features, EXTRA), F32),
        V((dps, 2, features, block), BF16), V((dps, 2, features, block), BF16),
        V((2, features, block), F32), V((2, features, block), BF16),
        V((2, 2, features, block), BF16),
        V((dps, rows_dp, first), BF16), V((dps, rows_dp, first), BF16),
        V((rows_dp, first), F32), V((dps - 1, rows_dp, first), BF16),
        V((experts, 2 * rows_own, first // 2), BF16), V((experts, 2 * rows_own, first // 2), BF16),
        V((features, second), BF16), V((features, second), BF16),
        V((experts, dps * rows_own, second), BF16),
        V((dps, 2 * rows_own, second // 2), BF16), V((dps, 2 * rows_own, second // 2), BF16),
        dma((2,)), dma((6,)), dma((2, 6)), dma((2, 2)), dma((2, 2, dps)), dma((2,)),
        dma((2, dps - 1)), dma((2,)),
        dma((2,)), dma((8,)), dma((2,)), dma((2,)), dma((2,)),
        dma((dps, 2)), dma((dps, 2)), dma((2,)), dma((2,)), dma((2, 2)), dma((2, 2)),
        dma((dps + 1,)), dma((dps + 1,)), dma((dps - 1,)), dma((dps - 1,)), dma, dma, dma, dma,
        dma((dps - 1,)), dma, dma((2,)),
    ]
    made = pl.pallas_call(
        partial(kernel, dims),
        out_shape=(
            out(tokens, micro, features, dtype=BF16),
            out(tokens, micro, features, dtype=BF16),
            out(2, 2, rows_own),
            out(rows_own, width),
            out(features, block),
            out(block, features),
        ),
        in_specs=[anywhere, anywhere, vmem, vmem, anywhere, anywhere, vmem, anywhere, anywhere, vmem],
        out_specs=(anywhere, anywhere, vmem, vmem, anywhere, anywhere),
        scratch_shapes=scratch,
        compiler_params=pltpu.CompilerParams(
            collective_id=0, has_side_effects=True, vmem_limit_bytes=62 * 2**20
        ),
        cost_estimate=pl.CostEstimate(
            flops=10_000_000_000, bytes_accessed=10_000_000, transcendentals=4_000_000
        ),
    )(
        inputs.transpose(1, 0, 2), cotangent.transpose(1, 0, 2), gains, biases, w_qkv, w_out,
        w_router.transpose(0, 2, 1), w_in, w_up, routes.transpose(0, 1, 3, 2),
    )
    outs, grads, *rest = pl.pallas_call(
        partial(finish, features),
        out_shape=(
            out(tokens, micro, features, dtype=BF16),
            out(tokens, micro, features, dtype=BF16),
            out(1, 2, rows_own),
            out(1, 2, rows_own),
            out(1, rows_own, 3 * features),
            out(1, rows_own, features),
            out(1, rows_own, experts),
            out(1, 1, features, block),
            out(1, 1, block, features),
        ),
        in_specs=[anywhere, anywhere, vmem, vmem, anywhere, anywhere],
        out_specs=(anywhere, anywhere, vmem, vmem, vmem, vmem, vmem, anywhere, anywhere),
        scratch_shapes=[
            V((features, block), F32), V((block, features), F32),
            V((tokens, micro, features), BF16), V((tokens, micro, features), BF16), dma((2, 4)),
        ],
    )(*made)
    return (
        outs.transpose(1, 0, 2)[None],
        grads.transpose(1, 0, 2)[None],
        *rest,
    )


def solution(mesh):
    sections, experts, dps = (mesh.shape[name] for name in ("section", "expert", "dp"))

    def run(*args):
        tokens, features = args[0].shape[1:]
        micro = args[0].shape[0]
        cap = 5 * tokens // (2 * experts) + 1
        ffs = args[7].shape[3] * dps
        dims = (sections, experts, dps, tokens, features, cap, ffs, micro)
        return local(dims, *args)

    return jax.shard_map(
        run,
        mesh=mesh,
        in_specs=(
            P(None, ("expert", "dp"), None),
            P(None, ("expert", "dp"), None),
            P("section", None, None),
            P("section", None, None),
            P("section", None, None),
            P("section", None, None),
            P("section", None, None),
            P("section", "expert", None, "dp"),
            P("section", "expert", "dp", None),
            P("section", None, ("expert", "dp"), None),
        ),
        out_specs=(
            P("section", None, ("expert", "dp"), None),
            P("section", None, ("expert", "dp"), None),
            P("section", None, ("expert", "dp")),
            P("section", None, ("expert", "dp")),
            P("section", ("expert", "dp"), None),
            P("section", ("expert", "dp"), None),
            P("section", ("expert", "dp"), None),
            P("section", "expert", None, "dp"),
            P("section", "expert", "dp", None),
        ),
        check_vma=False,
    )
```

```python
from functools import partial

import jax
import jax.numpy as jnp
from jax import lax
from jax.experimental import pallas as pl
from jax.experimental.pallas import tpu as pltpu
from jax.sharding import PartitionSpec as P

HEADS = 8
HEAD_DIM = 64
SEQ = 50
ROWS = 64
EPSILON = 1e-06
MESH = pl.DeviceIdType.MESH
F32 = jnp.float32
BF16 = jnp.bfloat16
EXTRA = 128
SIDE = 4
HOPS = (0, 1, 2, 1)
OFFSETS = sorted(
    ((y, z) for y in range(SIDE) for z in range(SIDE) if y or z),
    key=lambda at: -HOPS[at[0]] - HOPS[at[1]],
)


def nn(a, b):
    return lax.dot_general(a, b, (((1,), (0,)), ((), ())), preferred_element_type=F32)


def nt(a, b):
    return lax.dot_general(a, b, (((1,), (1,)), ((), ())), preferred_element_type=F32)


def tn(a, b):
    return lax.dot_general(a, b, (((0,), (0,)), ((), ())), preferred_element_type=F32)


def iota(shape, dim):
    return lax.broadcasted_iota(jnp.int32, shape, dim)


def split_sum(values):
    high = values.astype(BF16)
    return high, (values - high.astype(F32)).astype(BF16)


def normalized(values):
    center = values - jnp.mean(values, axis=-1, keepdims=True)
    root = lax.rsqrt(jnp.mean(center * center, axis=-1, keepdims=True) + EPSILON)
    return center * root, root


def norm_back(grad, norm, root, gain):
    scaled = grad * gain
    return root * (
        scaled
        - jnp.mean(scaled, axis=-1, keepdims=True)
        - norm * jnp.mean(scaled * norm, axis=-1, keepdims=True)
    )


def gelu_parts(x):
    z = jnp.abs(x) * 0.7071067811865476
    t = 1.0 / (1.0 + 0.3275911 * z)
    poly = t * (
        0.254829592 + t * (-0.284496736 + t * (1.421413741 + t * (-1.453152027 + t * 1.061405429)))
    )
    bell = jnp.exp(-z * z)
    tail = 0.5 * poly * bell
    share = jnp.where(x >= 0.0, 1.0 - tail, tail)
    return x * share, share + x * bell * 0.3989422804014327


def kernel(
    dims,
    inputs, cotangent, gains, biases, w_qkv, w_out, w_router, w_in, w_up, routes,
    o_outs, o_grads, o_norms, o_dense, o_in, o_up,
    xin, cot, rt, gn, bs, wq, wo, wr, wi, wu,
    place, s0, s1, m0, m1, wr128,
    states, norm1, packed, probs, blended, attended, norm2, shares,
    pick0, pick1, stage_out, stage_grad, join_out, join_grad,
    snd, rcv, rows_in, hidden, slope, acc, grows, gbuf, branch_kept, gblend, gpacked, small, extra_kept,
    part, part_in, part_acc, ring, ring_end,
    dense, dense_in, dense_acc, dense_dp, dense_out, dense_last,
    second, second_in, second_far, second_out, second_last, third, third_in, third_far,
    in_sem, w_send, w_recv, e_send, e_recv, r_send, f_send, t_send,
    a_send, a_recv, o_send, o_recv, o_loc,
    g_send, g_recv, h_send, h_recv, k_send, k_recv,
    d_send, d_recv, dx_send, dx_recv, dy_send, dy_recv, sy_send, sy_recv, sx_send, sx_recv, ty_send, ty_recv, fin_sem,
):
    sections, experts, dps, tokens, features, cap, ffs, micro = dims
    images = tokens // SEQ
    total = images * ROWS
    slots = experts * cap
    half = features // 2
    pairs = HEADS // 2
    span = 2 * HEAD_DIM
    rows_dp = features // dps
    rows_own = rows_dp // experts
    first_width = dense.shape[-1]
    second_width = second.shape[-1]
    scale = HEAD_DIM ** (-0.5)

    s = lax.axis_index("section")
    e = lax.axis_index("expert")
    d = lax.axis_index("dp")
    e_y, e_z = e // SIDE, lax.rem(e, SIDE)
    twin = (1 - s, e, d)

    def expert_at(y, z, sign=1):
        return (
            lax.rem(e_y + SIDE + sign * y, SIDE) * SIDE + lax.rem(e_z + SIDE + sign * z, SIDE)
        )

    def around(j):
        return lax.rem(d + j, dps)

    right, left, far = around(1), around(3), around(2)
    to_right, to_left, to_far = (s, e, right), (s, e, left), (s, e, far)

    def remote(src, dst, send, recv, device):
        return pltpu.make_async_remote_copy(
            src_ref=src, dst_ref=dst, send_sem=send, recv_sem=recv,
            device_id=device, device_id_type=MESH,
        )

    def arrived(ref, sem):
        pltpu.make_async_copy(ref, ref, sem).wait()

    def each(low, high, body):
        def step(j, carry):
            body(j)
            return carry
        lax.fori_loop(low, high, step, 0)

    barrier = pltpu.get_barrier_semaphore()
    pl.semaphore_signal(barrier, inc=1, device_id=twin, device_id_type=MESH)
    for device in (to_right, to_left, to_far):
        pl.semaphore_signal(barrier, inc=1, device_id=device, device_id_type=MESH)
    for y, z in OFFSETS:
        pl.semaphore_signal(
            barrier, inc=1, device_id=(s, expert_at(y, z), d), device_id_type=MESH
        )

    load_x = pltpu.make_async_copy(inputs, xin, in_sem.at[0])
    load_c = pltpu.make_async_copy(cotangent, cot, in_sem.at[1])
    load_x.start()
    dense_args = (
        (w_qkv, wq), (w_out, wo), (w_router, wr), (gains, gn), (biases, bs),
    )
    for i, (arg, kept) in enumerate(dense_args):
        pltpu.make_async_copy(arg.at[0], kept.at[s], w_recv.at[s, i]).start()
    pltpu.make_async_copy(routes.at[0, s], rt.at[s], w_recv.at[s, 5]).start()
    expert_args = ((w_in, wi), (w_up, wu))
    for i, (arg, kept) in enumerate(expert_args):
        pltpu.make_async_copy(arg.at[0, 0], kept.at[s, d], e_recv.at[i, s, d]).start()
    load_c.start()

    row = iota((total, tokens), 0)
    place[...] = jnp.where(
        ((row & (ROWS - 1)) < SEQ)
        & (iota((total, tokens), 1) == (row >> 6) * SEQ + (row & (ROWS - 1))),
        1.0, 0.0,
    ).astype(BF16)

    def own_micro(ref):
        both = ref[...].astype(F32)
        return jnp.where(s == 0, both[:, 0, :], both[:, 1, :]).astype(BF16)

    load_x.wait()
    states[0] = nn(place[...], own_micro(xin)).astype(BF16)
    small[...] = jnp.zeros_like(small)
    query_width = first_width - EXTRA
    rest_width = 3 * features - query_width
    second[:, rest_width:] = jnp.zeros((features, second_width - rest_width), BF16)

    pl.semaphore_wait(barrier, 1 + 3 + len(OFFSETS))

    def dense_copy(i):
        arg, kept = dense_args[i]
        return remote(arg.at[0], kept.at[s], w_send.at[i], w_recv.at[s, i], twin)

    def route_copy():
        return remote(routes.at[0, 1 - s], rt.at[s], w_send.at[5], w_recv.at[s, 5], twin)

    def expert_twin(i):
        arg, kept = expert_args[i]
        return remote(arg.at[0, 0], kept.at[s, d], t_send.at[i], e_recv.at[i, s, d], twin)

    def expert_next(i, way):
        arg, kept = expert_args[i]
        return remote(
            arg.at[0, 0], kept.at[s, d], e_send.at[i, way], e_recv.at[i, s, d],
            (to_right, to_left)[way],
        )

    def expert_relay(way):
        kept, other = ((wi, left), (wu, right))[way]
        return remote(
            kept.at[s, other], kept.at[s, other], r_send.at[way], e_recv.at[way, s, other],
            (to_right, to_left)[way],
        )

    def expert_forward(i, j):
        kept = expert_args[i][1]
        other = around(j)
        return remote(
            kept.at[s, other], kept.at[s, other], f_send.at[i, j - 1], e_recv.at[i, s, other], twin
        )

    def spread_experts():
        for i, way in ((0, 0), (1, 1), (1, 0), (0, 1)):
            expert_next(i, way).start()

    def relay(l):
        arrived(wi.at[l, left], e_recv.at[0, l, left])
        expert_relay(0).start()
        expert_forward(0, 3).start()
        arrived(wu.at[l, right], e_recv.at[1, l, right])
        expert_relay(1).start()
        expert_forward(1, 1).start()

    def relay_rest(l):
        arrived(wi.at[l, right], e_recv.at[0, l, right])
        expert_forward(0, 1).start()
        arrived(wu.at[l, left], e_recv.at[1, l, left])
        expert_forward(1, 3).start()

    for i in (3, 4, 0, 1, 2):
        dense_copy(i).start()
    route_copy().start()

    @pl.when(s == 0)
    def _():
        spread_experts()

    for i in range(2):
        expert_twin(i).start()

    live = (iota((total, 1), 0) & (ROWS - 1)) < SEQ

    def route(l):
        arrived(rt.at[l], w_recv.at[l, 5])
        named = nt(place[...], rt[l].astype(F32).astype(BF16))
        lane2 = iota((total, 2), 1)
        first = jnp.sum(jnp.where(lane2 == 0, named, 0.0), axis=1, keepdims=True)
        second = jnp.sum(jnp.where(lane2 == 1, named, 0.0), axis=1, keepdims=True)
        lane = iota((total, EXTRA), 1).astype(F32)
        hit0 = jnp.where(lane == jnp.where(live, first, -1.0), 1.0, 0.0)
        hit1 = jnp.where(lane == jnp.where(live, second, -1.0), 1.0, 0.0)
        below = jnp.where(iota((total, total), 1) < iota((total, total), 0), 1.0, 0.0).astype(BF16)
        before0 = nn(below, hit0.astype(BF16))
        before1 = nn(below, hit1.astype(BF16)) + jnp.sum(hit0, axis=0, keepdims=True)
        slot0 = first * cap + jnp.sum(hit0 * before0, axis=1, keepdims=True)
        slot1 = second * cap + jnp.sum(hit1 * before1, axis=1, keepdims=True)
        place_of = iota((total, slots), 1).astype(F32)
        s0[l] = jnp.where(place_of == jnp.where(live, slot0, -1.0), 1.0, 0.0).astype(BF16)
        s1[l] = jnp.where(place_of == jnp.where(live, slot1, -1.0), 1.0, 0.0).astype(BF16)
        m0[l] = hit0
        m1[l] = hit1

    def exchange_send(phase, way, values):
        blocks = values.reshape(experts, cap, features)
        snd[way] = jnp.concatenate(
            [blocks[:, :, :half], blocks[:, :, half:]], axis=1
        ).astype(BF16)
        for y, z in OFFSETS:
            peer = expert_at(y, z)
            remote(
                snd.at[way, peer], rcv.at[phase, e], a_send.at[way], a_recv.at[phase], (s, peer, d)
            ).start()
        pltpu.make_async_copy(snd.at[way, e], rcv.at[phase, e], a_recv.at[phase]).start()

    def exchange_recv(phase, way):
        arrived(rcv.at[phase], a_recv.at[phase])
        sent = snd.at[way, pl.ds(0, experts - 1)]
        arrived(sent, a_send.at[way])
        blocks = rcv[phase].astype(F32)
        blocks = jnp.concatenate([blocks[:, :cap], blocks[:, cap:]], axis=2)
        return blocks.reshape(slots, features).astype(BF16)

    def gate_parts(l):
        p = shares[l]
        hit0, hit1 = m0[l], m1[l]
        pair = jnp.sum(p * (hit0 + hit1), axis=1, keepdims=True)
        inverse = 1.0 / jnp.where(live, pair, 1.0)
        gate0 = jnp.sum(p * hit0, axis=1, keepdims=True) * inverse
        gate1 = jnp.sum(p * hit1, axis=1, keepdims=True) * inverse
        return p, hit0, hit1, inverse, gate0, gate1

    def out_copy(kind, l, stage):
        return remote(
            stage.at[l], (stage_out, stage_grad)[kind].at[2], o_send.at[kind], o_recv.at[kind], twin
        )

    def hand_out(kind, l, stage, values):
        stage[l] = tn(place[...], values).astype(BF16)

        @pl.when(s != l)
        def _():
            out_copy(kind, l, stage).start()

    def join(kind, stage, joined, dest):
        arrived(stage.at[2], o_recv.at[kind])
        own = stage[s].astype(F32)
        other = stage[2].astype(F32)
        joined[...] = jnp.stack(
            [jnp.where(s == 0, own, other), jnp.where(s == 0, other, own)], axis=1
        ).astype(BF16)
        return pltpu.make_async_copy(joined, dest, o_loc.at[kind])

    def pair_keys(ref_rows, side):
        return jnp.concatenate([ref_rows * side, ref_rows * (1.0 - side)], axis=0).astype(BF16)

    lane_side = jnp.where(iota((1, span), 1) < HEAD_DIM, 1.0, 0.0)
    in_left = iota((total, span), 1) < HEAD_DIM

    def attention(l):
        def need(*which):
            for i in which:
                arrived(dense_args[i][1].at[l], w_recv.at[l, i])
        need(3, 4)
        current = states[l].astype(F32)
        norm, _ = normalized(current)
        normed = (norm * gn[l, 0:1] + bs[l, 0:1]).astype(BF16)
        norm1[l] = normed
        need(0)
        packed[l] = nn(normed, wq[l]).astype(BF16)
        key_bias = jnp.where((iota((1, span), 1) & (ROWS - 1)) < SEQ, 0.0, -1e30)
        for p in range(pairs):
            at = p * span
            scores = jnp.concatenate([
                nt(
                    packed[l, i * ROWS:(i + 1) * ROWS, at:at + span],
                    pair_keys(packed[
                        l, i * ROWS:(i + 1) * ROWS, features + at:features + at + span
                    ].astype(F32), lane_side),
                )
                for i in range(images)
            ], axis=0) * scale + key_bias
            top0 = jnp.max(jnp.where(in_left, scores, -1e30), axis=-1, keepdims=True)
            top1 = jnp.max(jnp.where(in_left, -1e30, scores), axis=-1, keepdims=True)
            powers = jnp.exp(scores - jnp.where(in_left, top0, top1))
            sum0 = jnp.sum(jnp.where(in_left, powers, 0.0), axis=-1, keepdims=True)
            sum1 = jnp.sum(jnp.where(in_left, 0.0, powers), axis=-1, keepdims=True)
            prob = powers * jnp.where(in_left, 1.0 / sum0, 1.0 / sum1)
            probs[l, p] = prob
            low = prob.astype(BF16)
            for i in range(images):
                values = packed[
                    l, i * ROWS:(i + 1) * ROWS, 2 * features + at:2 * features + at + span
                ].astype(F32)
                blended[l, i * ROWS:(i + 1) * ROWS, at:at + span] = nn(
                    low[i * ROWS:(i + 1) * ROWS], pair_keys(values, lane_side)
                ).astype(BF16)
        need(1)
        middle = current + nn(blended[l], wo[l])
        attended[l] = middle
        norm, _ = normalized(middle)
        normed = (norm * gn[l, 1:2] + bs[l, 1:2]).astype(BF16)
        norm2[l] = normed
        exchange_send(4 * l, 0, tn(s0[l] + s1[l], normed))
        spread = jnp.where(iota((EXTRA, experts), 0) == iota((EXTRA, experts), 1), 1.0, 0.0)
        need(2)
        wr128[l] = nn(spread.astype(BF16), wr[l]).astype(BF16)
        logits = nt(normed, wr128[l])
        logits = jnp.where(iota((total, EXTRA), 1) < experts, logits, -1e30)
        logits = jnp.exp(logits - jnp.max(logits, axis=-1, keepdims=True))
        shares[l] = logits * (1.0 / jnp.sum(logits, axis=-1, keepdims=True))

    def block_at(step):
        return around(step + step // 2 - 2 * (step // 3))

    def expert_forward_pass(l):
        rows_in[l] = exchange_recv(4 * l, 0)
        acc[...] = jnp.zeros_like(acc)

        def block(step):
            b = block_at(step)

            @pl.when((s == l) & (step == 0))
            def _():
                for i, (_, kept) in enumerate(expert_args):
                    arrived(kept.at[l, d], e_recv.at[i, l, d])

            @pl.when((s == l) & (step == 3))
            def _():
                for i, (_, kept) in enumerate(expert_args):
                    arrived(kept.at[l, far], e_recv.at[i, l, far])
                    expert_forward(i, 2).start()

            @pl.when(s != l)
            def _():
                for i, (_, kept) in enumerate(expert_args):
                    arrived(kept.at[l, b], e_recv.at[i, l, b])

            after, dslope = gelu_parts(nn(rows_in[l], wi[l, b]))
            after = after.astype(BF16)
            hidden[l, b] = after
            slope[l, b] = dslope.astype(BF16)
            acc[...] += nn(after, wu[l, b])
        each(0, dps, block)
        exchange_send(4 * l + 1, 0, acc[...])

    def slot_grads(l, way, grad_y, gate0, gate1):
        exchange_send(
            4 * l + 2, way,
            tn(s0[l], (gate0 * grad_y).astype(BF16)) + tn(s1[l], (gate1 * grad_y).astype(BF16)),
        )

    def expert_backward_pass(l, way):
        grows[...] = exchange_recv(4 * l + 2, way)
        acc[...] = jnp.zeros_like(acc)

        def block(b):
            before = (nt(grows[...], wu[l, b]) * slope[l, b].astype(F32)).astype(BF16)
            slope[l, b] = before
            acc[...] += nt(before, wi[l, b])
        each(0, dps, block)
        exchange_send(4 * l + 3, way, acc[...])

    def part_copy(b, k):
        return remote(part.at[b, k], part_in.at[b, k], g_send.at[b, k], g_recv.at[b, k], twin)

    def expert_weights(l):
        def block(step):
            turn = 2 + step - 3 * (step // 2) - 2 * (step // 3)
            b, c = around(turn), around(dps - turn)
            part[b, 0] = tn(rows_in[l], slope[l, b]).astype(BF16)

            @pl.when(s != l)
            def _():
                part_copy(b, 0).start()

            part[c, 1] = tn(hidden[l, c], grows[...]).astype(BF16)

            @pl.when(s != l)
            def _():
                part_copy(c, 1).start()
        each(0, dps, block)

    def pair_part(b, k):
        arrived(part_in.at[b, k], g_recv.at[b, k])
        return part[b, k].astype(F32) + part_in[b, k].astype(F32)

    def ring_copy(k):
        return remote(
            part_in.at[far, k], ring.at[k], h_send.at[k], h_recv.at[k], (to_right, to_left)[k]
        )

    def ring_last(way, k):
        return remote(
            part_in.at[(right, left)[way], k], ring_end.at[way, k], k_send.at[way, k],
            k_recv.at[way, k], (to_right, to_left)[way],
        )

    def ring_first_step():
        for k in range(2):
            part_in[far, k] = pair_part(far, k).astype(BF16)
            ring_copy(k).start()
        for way, k in ((1, 0), (0, 1)):
            b = (right, left)[way]
            part_in[b, k] = pair_part(b, k).astype(BF16)
            ring_last(way, k).start()

    def ring_second_step():
        for way in range(2):
            b = (right, left)[way]
            value = pair_part(b, way)
            arrived(ring.at[way], h_recv.at[way])
            part_in[b, way] = (value + ring[way].astype(F32)).astype(BF16)
            ring_last(way, way).start()

    def ring_own():
        for k in range(2):
            part_acc[k] = pair_part(d, k)

    def ring_sent():
        for k in range(2):
            ring_copy(k).wait_send()
            for way in range(2):
                ring_last(way, k).wait_send()

    def part_sent():
        def done(b):
            for k in range(2):
                part_copy(b, k).wait_send()
        each(0, dps, done)

    def dense_twin(b):
        return remote(dense.at[b], dense_in.at[b], d_send.at[b], d_recv.at[b], twin)

    def dense_dp_copy(j):
        return remote(
            dense_in.at[around(j)], dense_dp.at[j - 1], dx_send.at[j - 1], dx_recv.at[j - 1],
            (s, e, around(j)),
        )

    def second_twin():
        return remote(second, second_in, d_send.at[dps], d_recv.at[dps], twin)

    def third_twin():
        return remote(third, third_in, d_send.at[dps + 1], d_recv.at[dps + 1], twin)

    def second_dp_copy(j):
        return remote(
            second_out.at[around(j)], second_last.at[d], sx_send.at[j - 1], sx_recv,
            (s, e, around(j)),
        )

    def narrow(values):
        half_width = values.shape[-1] // 2
        return jnp.concatenate(
            [values[:, :, :half_width], values[:, :, half_width:]], axis=1
        ).astype(BF16)

    def widen(values):
        return jnp.concatenate([values[:rows_own], values[rows_own:]], axis=1)

    def pair_rows(own, other, ends, send, recv):
        rows = rows_own * dps

        def pair(j):
            at = pl.ds(pl.multiple_of(j * rows, rows), rows)
            other[at] = (own[at].astype(F32) + other[at].astype(F32)).astype(BF16)
        each(0, experts, pair)
        for y, z in OFFSETS:
            peer = expert_at(y, z)
            at = pl.ds(pl.multiple_of(peer * rows, rows), rows)
            remote(other.at[at], ends.at[e], send, recv, (s, peer, d)).start()
        at = pl.ds(pl.multiple_of(e * rows, rows), rows)
        pltpu.make_async_copy(other.at[at], ends.at[e], recv).start()

    def pair_third():
        arrived(third_in, d_recv.at[dps + 1])
        pair_rows(third, third_in, third_far, ty_send, ty_recv)

    def pair_second():
        arrived(second_in, d_recv.at[dps])
        pair_rows(second, second_in, second_far, sy_send, sy_recv)

    def pair_first():
        for j in (2, 1, 3):
            other = around(j)
            arrived(dense_in.at[other], d_recv.at[other])
            dense_in[other] = (
                dense[other].astype(F32) + dense_in[other].astype(F32)
            ).astype(BF16)
            dense_dp_copy(j).start()
        arrived(dense_in.at[d], d_recv.at[d])
        dense_acc[...] = dense[d].astype(F32) + dense_in[d].astype(F32)

    def dense_middle():
        for j in (1, 3, 2):
            copy = dense_dp_copy(j)
            copy.wait_send()
            copy.wait_recv()
        summed = dense_acc[...]
        for j in range(dps - 1):
            summed = summed + dense_dp[j].astype(F32)
        dense_out[...] = narrow(summed.reshape(experts, rows_own, first_width))
        for y, z in OFFSETS:
            peer = expert_at(y, z)
            remote(
                dense_out.at[peer], dense_last.at[e], dy_send, dy_recv, (s, peer, d)
            ).start()
        pltpu.make_async_copy(dense_out.at[e], dense_last.at[e], dy_recv).start()
        arrived(third_far, ty_recv)
        arrived(third_in.at[pl.ds(0, features - rows_own * dps)], ty_send)
        late = third_far[0].astype(F32)
        for j in range(1, experts):
            late = late + third_far[j].astype(F32)
        arrived(second_far, sy_recv)
        arrived(second_in.at[pl.ds(0, features - rows_own * dps)], sy_send)
        summed = second_far[0].astype(F32)
        for j in range(1, experts):
            summed = summed + second_far[j].astype(F32)
        summed = jnp.concatenate([summed, late], axis=1)
        second_out[...] = narrow(summed.reshape(dps, rows_own, summed.shape[1]))
        for j in (2, 1, 3):
            second_dp_copy(j).start()
        pltpu.make_async_copy(second_out.at[d], second_last.at[d], sx_recv).start()

    def put(values, at):
        size = values.shape[1]
        blocks = values.reshape(experts, dps, rows_own, size)
        for b in range(dps):
            dense[b, :, pl.ds(at, size)] = blocks[:, b].reshape(rows_dp, size).astype(BF16)

    def put_extra(l):
        high, low = split_sum(small[l])
        lane = iota((8, EXTRA), 1)
        line = iota((8, EXTRA), 0)
        column = jnp.where((lane == line + experts) & (line < 4), 1.0, 0.0).astype(BF16)
        put(extra_kept[l] + tn(high, column) + tn(low, column), query_width)

    def put_third(l):
        third[...] = tn(blended[l], branch_kept[...]).astype(BF16)

        @pl.when(s != l)
        def _():
            third_twin().start()

    def put_second(l):
        second[:, :rest_width] = tn(norm1[l], gpacked[:, query_width:]).astype(BF16)

        @pl.when(s != l)
        def _():
            second_twin().start()

    def put_first(l):
        put(tn(norm1[l], gpacked[:, :query_width]), 0)
        put_extra(l)

        @pl.when(s != l)
        def _():
            for j in (2, 1, 3, 0):
                dense_twin(around(j)).start()

    def dense_twin_sent():
        third_twin().wait_send()
        second_twin().wait_send()
        for b in range(dps):
            dense_twin(b).wait_send()

    def gate_back(l, grad_y, gates):
        p, hit0, hit1, inverse, gate0, gate1 = gates
        gg0 = jnp.sum(grad_y * pick0[l].astype(F32), axis=1, keepdims=True)
        gg1 = jnp.sum(grad_y * pick1[l].astype(F32), axis=1, keepdims=True)
        mixed = gate0 * gg0 + gate1 * gg1
        q = (hit0 * (gg0 - mixed) + hit1 * (gg1 - mixed)) * inverse
        glog = p * (q - jnp.sum(p * q, axis=1, keepdims=True))
        high, low = split_sum(glog)
        extra_kept[l] = tn(norm2[l], high) + tn(norm2[l], low)
        return nn(high, wr128[l]) + nn(low, wr128[l])

    def attention_back(l, way, grad_y, from_gate, before, between):
        back = exchange_recv(4 * l + 3, way)
        grad_normed = nn(s0[l] + s1[l], back) + from_gate
        norm, root = normalized(attended[l])
        small[l, 0:1] = jnp.sum(grad_normed * norm, axis=0, keepdims=True)
        small[l, 1:2] = jnp.sum(grad_normed, axis=0, keepdims=True)
        grad_att = grad_y + norm_back(grad_normed, norm, root, gn[l, 1:2])
        branch = grad_att.astype(BF16)
        branch_kept[...] = branch
        before()
        gblend[...] = nt(branch, wo[l]).astype(BF16)
        for p in range(pairs):
            at = p * span
            queries = packed[l, :, at:at + span]
            keys = packed[l, :, features + at:features + at + span]
            values = packed[l, :, 2 * features + at:2 * features + at + span]
            prob = probs[l, p]
            low = prob.astype(BF16)
            grad_prob = jnp.concatenate([
                nt(
                    gblend[i * ROWS:(i + 1) * ROWS, at:at + span],
                    pair_keys(values[i * ROWS:(i + 1) * ROWS].astype(F32), lane_side),
                )
                for i in range(images)
            ], axis=0)
            mixed = prob * grad_prob
            sum0 = jnp.sum(jnp.where(in_left, mixed, 0.0), axis=-1, keepdims=True)
            sum1 = jnp.sum(jnp.where(in_left, 0.0, mixed), axis=-1, keepdims=True)
            grad_score = (prob * (grad_prob - jnp.where(in_left, sum0, sum1))).astype(BF16)
            for i in range(images):
                rows = slice(i * ROWS, (i + 1) * ROWS)
                one = grad_score[rows]
                grad_query = nn(one, pair_keys(keys[rows].astype(F32), lane_side)) * scale
                grad_key = tn(one, queries[rows]) * scale
                grad_value = tn(low[rows], gblend[rows, at:at + span])
                side = in_left[:ROWS]
                grad_key = jnp.where(side, grad_key[:ROWS], grad_key[ROWS:])
                grad_value = jnp.where(side, grad_value[:ROWS], grad_value[ROWS:])
                gpacked[rows, at:at + span] = grad_query.astype(BF16)
                gpacked[rows, features + at:features + at + span] = grad_key.astype(BF16)
                gpacked[rows, 2 * features + at:2 * features + at + span] = grad_value.astype(BF16)
        between()
        grad_normed = nt(gpacked[...], wq[l])
        norm, root = normalized(states[l].astype(F32))
        small[l, 2:3] = jnp.sum(grad_normed * norm, axis=0, keepdims=True)
        small[l, 3:4] = jnp.sum(grad_normed, axis=0, keepdims=True)
        return grad_att, grad_normed, norm, root

    def finish_back(l, grad_att, grad_normed, norm, root):
        gbuf[...] = (grad_att + norm_back(grad_normed, norm, root, gn[l, 0:1])).astype(BF16)

    def combine(l, gate0, gate1, way):
        back = exchange_recv(4 * l + 1, way)
        picked0 = nn(s0[l], back)
        picked1 = nn(s1[l], back)
        pick0[l] = picked0.astype(BF16)
        pick1[l] = picked1.astype(BF16)
        states[l + 1] = (attended[l] + gate0 * picked0 + gate1 * picked1).astype(BF16)

    route(0)
    attention(0)

    @pl.when(s == 0)
    def _():
        relay(0)
        relay_rest(0)

    route(1)
    expert_forward_pass(0)

    @pl.when(s == 1)
    def _():
        spread_experts()

    load_c.wait()
    gbuf[...] = nn(place[...], own_micro(cot)).astype(BF16)
    gates = gate_parts(0)
    combine(0, gates[4], gates[5], 0)

    @pl.when(s == 1)
    def _():
        relay(1)

    attention(1)
    gates = gate_parts(1)
    grad_y = gbuf[...].astype(F32)
    slot_grads(1, 1, grad_y, gates[4], gates[5])

    @pl.when(s == 1)
    def _():
        relay_rest(1)

    hand_out(0, 0, stage_out, states[1])
    expert_forward_pass(1)
    expert_backward_pass(1, 1)
    expert_weights(1)
    combine(1, gates[4], gates[5], 0)
    from_gate = gate_back(1, grad_y, gates)

    @pl.when(s == 1)
    def _():
        ring_first_step()

    kept = attention_back(1, 1, grad_y, from_gate, lambda: None, lambda: None)
    finish_back(1, *kept)

    gates = gate_parts(0)
    grad_y = gbuf[...].astype(F32)
    slot_grads(0, 0, grad_y, gates[4], gates[5])
    put_third(1)
    put_second(1)
    put_first(1)

    @pl.when(s == 1)
    def _():
        ring_second_step()
        ring_own()

    hand_out(0, 1, stage_out, states[2])
    hand_out(1, 1, stage_grad, gbuf[...])
    from_gate = gate_back(0, grad_y, gates)
    expert_backward_pass(0, 0)

    @pl.when(s == 0)
    def _():
        part_sent()

    expert_weights(0)

    @pl.when(s == 0)
    def _():
        ring_first_step()
        dense_twin_sent()

    @pl.when(s == 1)
    def _():
        pair_third()
        pair_second()
        pair_first()

    def between():
        put_second(0)

        @pl.when(s == 0)
        def _():
            ring_second_step()
            pair_third()
            pair_second()

    kept = attention_back(0, 0, grad_y, from_gate, lambda: put_third(0), between)
    put_first(0)

    @pl.when(s == 0)
    def _():
        pair_first()

    finish_back(0, *kept)
    hand_out(1, 0, stage_grad, gbuf[...])
    keep_out = join(0, stage_out, join_out, o_outs)
    keep_out.start()

    @pl.when(s == 0)
    def _():
        ring_own()

    dense_middle()

    for k in range(2):
        for way in range(2):
            arrived(ring_end.at[way, k], k_recv.at[way, k])
            part_acc[k] += ring_end[way, k].astype(F32)
    keep_in = pltpu.make_async_copy(part_acc.at[0], o_in, fin_sem.at[0])
    keep_up = pltpu.make_async_copy(part_acc.at[1], o_up, fin_sem.at[1])
    keep_in.start()
    keep_up.start()
    keep_grad = join(1, stage_grad, join_grad, o_grads)
    keep_grad.start()

    arrived(dense_last, dy_recv)
    arrived(second_last, sx_recv)
    final = jnp.concatenate([
        widen(jnp.sum(dense_last[...].astype(F32), axis=0)),
        widen(jnp.sum(second_last[...].astype(F32), axis=0)),
    ], axis=1)
    o_dense[...] = final
    tail = final[:, query_width:first_width]
    tail_high, tail_low = split_sum(tail)
    tail_low, tail_rest = split_sum(tail - tail_high.astype(F32))

    def column_rows(late, early):
        lane = iota((2, EXTRA), 1)
        line = iota((2, EXTRA), 0)
        wanted = jnp.where(line == 0, experts + early, experts + late)
        pick = jnp.where(lane == wanted, 1.0, 0.0).astype(BF16)
        return nt(pick, tail_high) + nt(pick, tail_low) + nt(pick, tail_rest)

    o_norms[0] = column_rows(0, 2)
    o_norms[1] = column_rows(1, 3)

    for i in range(5):
        dense_copy(i).wait_send()
    route_copy().wait_send()
    for i in range(2):
        expert_twin(i).wait_send()
        expert_relay(i).wait_send()
        for way in range(2):
            expert_next(i, way).wait_send()
        for j in range(1, dps):
            expert_forward(i, j).wait_send()

    ring_sent()

    @pl.when(s == 1)
    def _():
        part_sent()
        dense_twin_sent()

    out_copy(0, 1 - s, stage_out).wait_send()
    out_copy(1, 1 - s, stage_grad).wait_send()
    arrived(dense_out.at[pl.ds(0, experts - 1)], dy_send)
    for j in range(1, dps):
        second_dp_copy(j).wait_send()
    keep_out.wait()
    keep_grad.wait()
    keep_in.wait()
    keep_up.wait()


def finish(
    features, outs, grads, norms, dense, part_in, part_up,
    o_outs, o_grads, o_gain, o_bias, o_qkv, o_attn, o_router, o_in, o_up,
    v_in, v_up, v_outs, v_grads, sems,
):
    passes = (
        (part_in, v_in, o_in.at[0, 0]), (part_up, v_up, o_up.at[0, 0]),
        (outs, v_outs, o_outs), (grads, v_grads, o_grads),
    )
    loads = [
        pltpu.make_async_copy(source, kept, sems.at[0, i])
        for i, (source, kept, _) in enumerate(passes)
    ]
    copies = [
        pltpu.make_async_copy(kept, dest, sems.at[1, i])
        for i, (_, kept, dest) in enumerate(passes)
    ]
    for load in loads:
        load.start()
    o_gain[0] = norms[0]
    o_bias[0] = norms[1]
    width = dense.shape[-1]
    first = width * 2 // 9
    query = first - EXTRA
    o_qkv[0, :, :query] = dense[:, :query]
    o_qkv[0, :, query:] = dense[:, first: first + 3 * features - query]
    o_attn[0] = dense[:, width - features:]
    o_router[0] = dense[:, query: query + o_router.shape[-1]]
    for load, copy in zip(loads, copies):
        load.wait()
        copy.start()
    for copy in copies:
        copy.wait()


def local(
    dims, inputs, cotangent, gains, biases, w_qkv, w_out, w_router, w_in, w_up, routes
):
    sections, experts, dps, tokens, features, cap, ffs, micro = dims
    images = tokens // SEQ
    total = images * ROWS
    slots = experts * cap
    rows_dp = features // dps
    rows_own = rows_dp // experts
    width = -(-(4 * features + EXTRA) // 256) * 256
    first = width * 2 // 9
    second = width - first
    half = features // 2
    block = ffs // dps
    dma = pltpu.SemaphoreType.DMA
    anywhere = pl.BlockSpec(memory_space=pl.ANY)
    vmem = pl.BlockSpec(memory_space=pltpu.VMEM)

    def out(*shape, dtype=F32):
        return jax.ShapeDtypeStruct(shape, dtype)

    V = pltpu.VMEM
    pairs, span = HEADS // 2, 2 * HEAD_DIM
    scratch = [
        V((tokens, 2, features), BF16), V((tokens, 2, features), BF16),
        V((2, 2, tokens), jnp.int32),
        V((2, 2, features), F32), V((2, 2, features), F32),
        V((2, features, 3 * features), BF16), V((2, features, features), BF16),
        V((2, experts, features), BF16),
        V((2, dps, features, block), BF16), V((2, dps, block, features), BF16),
        V((total, tokens), BF16),
        V((2, total, slots), BF16), V((2, total, slots), BF16),
        V((2, total, EXTRA), F32), V((2, total, EXTRA), F32), V((2, EXTRA, features), BF16),
        V((3, total, features), BF16), V((2, total, features), BF16),
        V((2, total, 3 * features), BF16), V((2, pairs, total, span), F32),
        V((2, total, features), BF16), V((2, total, features), F32),
        V((2, total, features), BF16), V((2, total, EXTRA), F32),
        V((2, total, features), BF16), V((2, total, features), BF16),
        V((3, tokens, features), BF16), V((3, tokens, features), BF16),
        V((tokens, 2, features), BF16), V((tokens, 2, features), BF16),
        V((2, experts, 2 * cap, half), BF16), V((8, experts, 2 * cap, half), BF16),
        V((2, slots, features), BF16),
        V((2, dps, slots, block), BF16), V((2, dps, slots, block), BF16),
        V((slots, features), F32), V((slots, features), BF16),
        V((total, features), BF16), V((total, features), BF16), V((total, features), BF16),
        V((total, 3 * features), BF16),
        V((2, 8, features), F32), V((2, features, EXTRA), F32),
        V((dps, 2, features, block), BF16), V((dps, 2, features, block), BF16),
        V((2, features, block), F32), V((2, features, block), BF16),
        V((2, 2, features, block), BF16),
        V((dps, rows_dp, first), BF16), V((dps, rows_dp, first), BF16),
        V((rows_dp, first), F32), V((dps - 1, rows_dp, first), BF16),
        V((experts, 2 * rows_own, first // 2), BF16), V((experts, 2 * rows_own, first // 2), BF16),
        V((features, second - features), BF16), V((features, second - features), BF16),
        V((experts, dps * rows_own, second - features), BF16),
        V((dps, 2 * rows_own, second // 2), BF16), V((dps, 2 * rows_own, second // 2), BF16),
        V((features, features), BF16), V((features, features), BF16),
        V((experts, dps * rows_own, features), BF16),
        dma((2,)), dma((6,)), dma((2, 6)), dma((2, 2)), dma((2, 2, dps)), dma((2,)),
        dma((2, dps - 1)), dma((2,)),
        dma((2,)), dma((8,)), dma((2,)), dma((2,)), dma((2,)),
        dma((dps, 2)), dma((dps, 2)), dma((2,)), dma((2,)), dma((2, 2)), dma((2, 2)),
        dma((dps + 2,)), dma((dps + 2,)), dma((dps - 1,)), dma((dps - 1,)), dma, dma, dma, dma,
        dma((dps - 1,)), dma, dma, dma, dma((2,)),
    ]
    made = pl.pallas_call(
        partial(kernel, dims),
        out_shape=(
            out(tokens, micro, features, dtype=BF16),
            out(tokens, micro, features, dtype=BF16),
            out(2, 2, rows_own),
            out(rows_own, width),
            out(features, block),
            out(block, features),
        ),
        in_specs=[anywhere, anywhere, vmem, vmem, anywhere, anywhere, vmem, anywhere, anywhere, vmem],
        out_specs=(anywhere, anywhere, vmem, vmem, anywhere, anywhere),
        scratch_shapes=scratch,
        compiler_params=pltpu.CompilerParams(
            collective_id=0, has_side_effects=True, vmem_limit_bytes=62 * 2**20
        ),
        cost_estimate=pl.CostEstimate(
            flops=10_000_000_000, bytes_accessed=10_000_000, transcendentals=4_000_000
        ),
    )(
        inputs.transpose(1, 0, 2), cotangent.transpose(1, 0, 2), gains, biases, w_qkv, w_out,
        w_router.transpose(0, 2, 1), w_in, w_up, routes.transpose(0, 1, 3, 2),
    )
    outs, grads, *rest = pl.pallas_call(
        partial(finish, features),
        out_shape=(
            out(tokens, micro, features, dtype=BF16),
            out(tokens, micro, features, dtype=BF16),
            out(1, 2, rows_own),
            out(1, 2, rows_own),
            out(1, rows_own, 3 * features),
            out(1, rows_own, features),
            out(1, rows_own, experts),
            out(1, 1, features, block),
            out(1, 1, block, features),
        ),
        in_specs=[anywhere, anywhere, vmem, vmem, anywhere, anywhere],
        out_specs=(anywhere, anywhere, vmem, vmem, vmem, vmem, vmem, anywhere, anywhere),
        scratch_shapes=[
            V((features, block), F32), V((block, features), F32),
            V((tokens, micro, features), BF16), V((tokens, micro, features), BF16), dma((2, 4)),
        ],
    )(*made)
    return (
        outs.transpose(1, 0, 2)[None],
        grads.transpose(1, 0, 2)[None],
        *rest,
    )


def solution(mesh):
    sections, experts, dps = (mesh.shape[name] for name in ("section", "expert", "dp"))

    def run(*args):
        tokens, features = args[0].shape[1:]
        micro = args[0].shape[0]
        cap = 5 * tokens // (2 * experts) + 1
        ffs = args[7].shape[3] * dps
        dims = (sections, experts, dps, tokens, features, cap, ffs, micro)
        return local(dims, *args)

    return jax.shard_map(
        run,
        mesh=mesh,
        in_specs=(
            P(None, ("expert", "dp"), None),
            P(None, ("expert", "dp"), None),
            P("section", None, None),
            P("section", None, None),
            P("section", None, None),
            P("section", None, None),
            P("section", None, None),
            P("section", "expert", None, "dp"),
            P("section", "expert", "dp", None),
            P("section", None, ("expert", "dp"), None),
        ),
        out_specs=(
            P("section", None, ("expert", "dp"), None),
            P("section", None, ("expert", "dp"), None),
            P("section", None, ("expert", "dp")),
            P("section", None, ("expert", "dp")),
            P("section", ("expert", "dp"), None),
            P("section", ("expert", "dp"), None),
            P("section", ("expert", "dp"), None),
            P("section", "expert", None, "dp"),
            P("section", "expert", "dp", None),
        ),
        check_vma=False,
    )
```

```python
from functools import partial

import jax
import jax.numpy as jnp
from jax import lax
from jax.experimental import pallas as pl
from jax.experimental.pallas import tpu as pltpu
from jax.sharding import PartitionSpec as P

HEADS = 8
HEAD_DIM = 64
SEQ = 50
ROWS = 64
EPSILON = 1e-06
MESH = pl.DeviceIdType.MESH
F32 = jnp.float32
BF16 = jnp.bfloat16
EXTRA = 128
SIDE = 4
HOPS = (0, 1, 2, 1)
OFFSETS = sorted(
    ((y, z) for y in range(SIDE) for z in range(SIDE) if y or z),
    key=lambda at: -HOPS[at[0]] - HOPS[at[1]],
)


def nn(a, b):
    return lax.dot_general(a, b, (((1,), (0,)), ((), ())), preferred_element_type=F32)


def nt(a, b):
    return lax.dot_general(a, b, (((1,), (1,)), ((), ())), preferred_element_type=F32)


def tn(a, b):
    return lax.dot_general(a, b, (((0,), (0,)), ((), ())), preferred_element_type=F32)


def iota(shape, dim):
    return lax.broadcasted_iota(jnp.int32, shape, dim)


def split_sum(values):
    high = values.astype(BF16)
    return high, (values - high.astype(F32)).astype(BF16)


def normalized(values):
    center = values - jnp.mean(values, axis=-1, keepdims=True)
    root = lax.rsqrt(jnp.mean(center * center, axis=-1, keepdims=True) + EPSILON)
    return center * root, root


def norm_back(grad, norm, root, gain):
    scaled = grad * gain
    return root * (
        scaled
        - jnp.mean(scaled, axis=-1, keepdims=True)
        - norm * jnp.mean(scaled * norm, axis=-1, keepdims=True)
    )


def gelu_parts(x):
    z = jnp.abs(x) * 0.7071067811865476
    t = 1.0 / (1.0 + 0.3275911 * z)
    poly = t * (
        0.254829592 + t * (-0.284496736 + t * (1.421413741 + t * (-1.453152027 + t * 1.061405429)))
    )
    bell = jnp.exp(-z * z)
    tail = 0.5 * poly * bell
    share = jnp.where(x >= 0.0, 1.0 - tail, tail)
    return x * share, share + x * bell * 0.3989422804014327


def kernel(
    dims,
    inputs, cotangent, gains, biases, w_qkv, w_out, w_router, w_in, w_up, routes,
    o_outs, o_grads, o_norms, o_dense, o_in, o_up,
    xin, cot, rt, gn, bs, wq, wo, wr, wi, wu,
    place, s0, s1, m0, m1, wr128,
    states, norm1, packed, probs, blended, attended, norm2, shares,
    pick0, pick1, stage_out, stage_grad, join_out, join_grad,
    snd, rcv, rows_in, hidden, slope, acc, grows, gbuf, branch_kept, gblend, gpacked, small, extra_kept,
    part, part_in, part_acc, ring, ring_end,
    dense, dense_in, dense_acc, dense_dp, dense_out, dense_last,
    second, second_in, second_far, second_out, second_last, third, third_in, third_far,
    in_sem, w_send, w_recv, e_send, e_recv, r_send, f_send, t_send,
    a_send, a_recv, o_send, o_recv, o_loc,
    g_send, g_recv, h_send, h_recv, k_send, k_recv,
    d_send, d_recv, dx_send, dx_recv, dy_send, dy_recv, sy_send, sy_recv, sx_send, sx_recv, ty_send, ty_recv, fin_sem,
):
    sections, experts, dps, tokens, features, cap, ffs, micro = dims
    images = tokens // SEQ
    total = images * ROWS
    slots = experts * cap
    half = features // 2
    pairs = HEADS // 2
    span = 2 * HEAD_DIM
    rows_dp = features // dps
    rows_own = rows_dp // experts
    first_width = dense.shape[-1]
    second_width = second.shape[-1]
    scale = HEAD_DIM ** (-0.5)

    s = lax.axis_index("section")
    e = lax.axis_index("expert")
    d = lax.axis_index("dp")
    e_y, e_z = e // SIDE, lax.rem(e, SIDE)
    twin = (1 - s, e, d)

    def expert_at(y, z, sign=1):
        return (
            lax.rem(e_y + SIDE + sign * y, SIDE) * SIDE + lax.rem(e_z + SIDE + sign * z, SIDE)
        )

    def around(j):
        return lax.rem(d + j, dps)

    right, left, far = around(1), around(3), around(2)
    to_right, to_left, to_far = (s, e, right), (s, e, left), (s, e, far)

    def remote(src, dst, send, recv, device):
        return pltpu.make_async_remote_copy(
            src_ref=src, dst_ref=dst, send_sem=send, recv_sem=recv,
            device_id=device, device_id_type=MESH,
        )

    def arrived(ref, sem):
        pltpu.make_async_copy(ref, ref, sem).wait()

    def each(low, high, body):
        def step(j, carry):
            body(j)
            return carry
        lax.fori_loop(low, high, step, 0)

    barrier = pltpu.get_barrier_semaphore()
    pl.semaphore_signal(barrier, inc=1, device_id=twin, device_id_type=MESH)
    for device in (to_right, to_left, to_far):
        pl.semaphore_signal(barrier, inc=1, device_id=device, device_id_type=MESH)
    for y, z in OFFSETS:
        pl.semaphore_signal(
            barrier, inc=1, device_id=(s, expert_at(y, z), d), device_id_type=MESH
        )

    load_x = pltpu.make_async_copy(inputs, xin, in_sem.at[0])
    load_c = pltpu.make_async_copy(cotangent, cot, in_sem.at[1])
    load_x.start()
    dense_args = (
        (w_qkv, wq), (w_out, wo), (w_router, wr), (gains, gn), (biases, bs),
    )
    for i, (arg, kept) in enumerate(dense_args):
        pltpu.make_async_copy(arg.at[0], kept.at[s], w_recv.at[s, i]).start()
    pltpu.make_async_copy(routes.at[0, s], rt.at[s], w_recv.at[s, 5]).start()
    expert_args = ((w_in, wi), (w_up, wu))
    for i, (arg, kept) in enumerate(expert_args):
        pltpu.make_async_copy(arg.at[0, 0], kept.at[s, d], e_recv.at[i, s, d]).start()
    load_c.start()

    row = iota((total, tokens), 0)
    place[...] = jnp.where(
        ((row & (ROWS - 1)) < SEQ)
        & (iota((total, tokens), 1) == (row >> 6) * SEQ + (row & (ROWS - 1))),
        1.0, 0.0,
    ).astype(BF16)

    def own_micro(ref):
        both = ref[...].astype(F32)
        return jnp.where(s == 0, both[:, 0, :], both[:, 1, :]).astype(BF16)

    load_x.wait()
    states[0] = nn(place[...], own_micro(xin)).astype(BF16)
    small[...] = jnp.zeros_like(small)
    query_width = first_width - EXTRA
    rest_width = 3 * features - query_width
    second[:, rest_width:] = jnp.zeros((features, second_width - rest_width), BF16)

    pl.semaphore_wait(barrier, 1 + 3 + len(OFFSETS))

    def dense_copy(i):
        arg, kept = dense_args[i]
        return remote(arg.at[0], kept.at[s], w_send.at[i], w_recv.at[s, i], twin)

    def route_copy():
        return remote(routes.at[0, 1 - s], rt.at[s], w_send.at[5], w_recv.at[s, 5], twin)

    def expert_twin(i):
        arg, kept = expert_args[i]
        return remote(arg.at[0, 0], kept.at[s, d], t_send.at[i], e_recv.at[i, s, d], twin)

    def expert_next(i, way):
        arg, kept = expert_args[i]
        return remote(
            arg.at[0, 0], kept.at[s, d], e_send.at[i, way], e_recv.at[i, s, d],
            (to_right, to_left)[way],
        )

    def expert_relay(way):
        kept, other = ((wi, left), (wu, right))[way]
        return remote(
            kept.at[s, other], kept.at[s, other], r_send.at[way], e_recv.at[way, s, other],
            (to_right, to_left)[way],
        )

    def expert_forward(i, j):
        kept = expert_args[i][1]
        other = around(j)
        return remote(
            kept.at[s, other], kept.at[s, other], f_send.at[i, j - 1], e_recv.at[i, s, other], twin
        )

    def spread_experts():
        for i, way in ((0, 0), (1, 1), (1, 0), (0, 1)):
            expert_next(i, way).start()

    def relay(l):
        arrived(wi.at[l, left], e_recv.at[0, l, left])
        expert_relay(0).start()
        expert_forward(0, 3).start()
        arrived(wu.at[l, right], e_recv.at[1, l, right])
        expert_relay(1).start()
        expert_forward(1, 1).start()

    def relay_rest(l):
        arrived(wi.at[l, right], e_recv.at[0, l, right])
        expert_forward(0, 1).start()
        arrived(wu.at[l, left], e_recv.at[1, l, left])
        expert_forward(1, 3).start()

    for i in (3, 4, 0, 1, 2):
        dense_copy(i).start()
    route_copy().start()

    @pl.when(s == 0)
    def _():
        spread_experts()

    for i in range(2):
        expert_twin(i).start()

    live = (iota((total, 1), 0) & (ROWS - 1)) < SEQ

    def route(l):
        arrived(rt.at[l], w_recv.at[l, 5])
        named = nt(place[...], rt[l].astype(F32).astype(BF16))
        lane2 = iota((total, 2), 1)
        first = jnp.sum(jnp.where(lane2 == 0, named, 0.0), axis=1, keepdims=True)
        second = jnp.sum(jnp.where(lane2 == 1, named, 0.0), axis=1, keepdims=True)
        lane = iota((total, EXTRA), 1).astype(F32)
        hit0 = jnp.where(lane == jnp.where(live, first, -1.0), 1.0, 0.0)
        hit1 = jnp.where(lane == jnp.where(live, second, -1.0), 1.0, 0.0)
        below = jnp.where(iota((total, total), 1) < iota((total, total), 0), 1.0, 0.0).astype(BF16)
        before0 = nn(below, hit0.astype(BF16))
        before1 = nn(below, hit1.astype(BF16)) + jnp.sum(hit0, axis=0, keepdims=True)
        slot0 = first * cap + jnp.sum(hit0 * before0, axis=1, keepdims=True)
        slot1 = second * cap + jnp.sum(hit1 * before1, axis=1, keepdims=True)
        place_of = iota((total, slots), 1).astype(F32)
        s0[l] = jnp.where(place_of == jnp.where(live, slot0, -1.0), 1.0, 0.0).astype(BF16)
        s1[l] = jnp.where(place_of == jnp.where(live, slot1, -1.0), 1.0, 0.0).astype(BF16)
        m0[l] = hit0
        m1[l] = hit1

    def exchange_send(phase, way, values):
        blocks = values.reshape(experts, cap, features)
        snd[way] = jnp.concatenate(
            [blocks[:, :, :half], blocks[:, :, half:]], axis=1
        ).astype(BF16)
        for y, z in OFFSETS:
            peer = expert_at(y, z)
            remote(
                snd.at[way, peer], rcv.at[phase, e], a_send.at[way], a_recv.at[phase], (s, peer, d)
            ).start()
        pltpu.make_async_copy(snd.at[way, e], rcv.at[phase, e], a_recv.at[phase]).start()

    def exchange_recv(phase, way):
        arrived(rcv.at[phase], a_recv.at[phase])
        sent = snd.at[way, pl.ds(0, experts - 1)]
        arrived(sent, a_send.at[way])
        blocks = rcv[phase].astype(F32)
        blocks = jnp.concatenate([blocks[:, :cap], blocks[:, cap:]], axis=2)
        return blocks.reshape(slots, features).astype(BF16)

    def gate_parts(l):
        p = shares[l]
        hit0, hit1 = m0[l], m1[l]
        pair = jnp.sum(p * (hit0 + hit1), axis=1, keepdims=True)
        inverse = 1.0 / jnp.where(live, pair, 1.0)
        gate0 = jnp.sum(p * hit0, axis=1, keepdims=True) * inverse
        gate1 = jnp.sum(p * hit1, axis=1, keepdims=True) * inverse
        return p, hit0, hit1, inverse, gate0, gate1

    def out_copy(kind, l, stage):
        return remote(
            stage.at[l], (stage_out, stage_grad)[kind].at[2], o_send.at[kind], o_recv.at[kind], twin
        )

    def hand_out(kind, l, stage, values):
        stage[l] = tn(place[...], values).astype(BF16)

        @pl.when(s != l)
        def _():
            out_copy(kind, l, stage).start()

    def join(kind, stage, joined, dest):
        arrived(stage.at[2], o_recv.at[kind])
        own = stage[s].astype(F32)
        other = stage[2].astype(F32)
        joined[...] = jnp.stack(
            [jnp.where(s == 0, own, other), jnp.where(s == 0, other, own)], axis=1
        ).astype(BF16)
        return pltpu.make_async_copy(joined, dest, o_loc.at[kind])

    def pair_keys(ref_rows, side):
        return jnp.concatenate([ref_rows * side, ref_rows * (1.0 - side)], axis=0).astype(BF16)

    lane_side = jnp.where(iota((1, span), 1) < HEAD_DIM, 1.0, 0.0)
    in_left = iota((total, span), 1) < HEAD_DIM

    def attention(l):
        def need(*which):
            for i in which:
                arrived(dense_args[i][1].at[l], w_recv.at[l, i])
        need(3, 4)
        current = states[l].astype(F32)
        norm, _ = normalized(current)
        normed = (norm * gn[l, 0:1] + bs[l, 0:1]).astype(BF16)
        norm1[l] = normed
        need(0)
        packed[l] = nn(normed, wq[l]).astype(BF16)
        key_bias = jnp.where((iota((1, span), 1) & (ROWS - 1)) < SEQ, 0.0, -1e30)
        for p in range(pairs):
            at = p * span
            scores = jnp.concatenate([
                nt(
                    packed[l, i * ROWS:(i + 1) * ROWS, at:at + span],
                    pair_keys(packed[
                        l, i * ROWS:(i + 1) * ROWS, features + at:features + at + span
                    ].astype(F32), lane_side),
                )
                for i in range(images)
            ], axis=0) * scale + key_bias
            top0 = jnp.max(jnp.where(in_left, scores, -1e30), axis=-1, keepdims=True)
            top1 = jnp.max(jnp.where(in_left, -1e30, scores), axis=-1, keepdims=True)
            powers = jnp.exp(scores - jnp.where(in_left, top0, top1))
            sum0 = jnp.sum(jnp.where(in_left, powers, 0.0), axis=-1, keepdims=True)
            sum1 = jnp.sum(jnp.where(in_left, 0.0, powers), axis=-1, keepdims=True)
            prob = powers * jnp.where(in_left, 1.0 / sum0, 1.0 / sum1)
            probs[l, p] = prob
            low = prob.astype(BF16)
            for i in range(images):
                values = packed[
                    l, i * ROWS:(i + 1) * ROWS, 2 * features + at:2 * features + at + span
                ].astype(F32)
                blended[l, i * ROWS:(i + 1) * ROWS, at:at + span] = nn(
                    low[i * ROWS:(i + 1) * ROWS], pair_keys(values, lane_side)
                ).astype(BF16)
        need(1)
        middle = current + nn(blended[l], wo[l])
        attended[l] = middle
        norm, _ = normalized(middle)
        normed = (norm * gn[l, 1:2] + bs[l, 1:2]).astype(BF16)
        norm2[l] = normed
        exchange_send(4 * l, 0, tn(s0[l] + s1[l], normed))
        spread = jnp.where(iota((EXTRA, experts), 0) == iota((EXTRA, experts), 1), 1.0, 0.0)
        need(2)
        wr128[l] = nn(spread.astype(BF16), wr[l]).astype(BF16)
        logits = nt(normed, wr128[l])
        logits = jnp.where(iota((total, EXTRA), 1) < experts, logits, -1e30)
        logits = jnp.exp(logits - jnp.max(logits, axis=-1, keepdims=True))
        shares[l] = logits * (1.0 / jnp.sum(logits, axis=-1, keepdims=True))

    def block_at(step):
        return around(step + step // 2 - 2 * (step // 3))

    def expert_forward_pass(l):
        rows_in[l] = exchange_recv(4 * l, 0)
        order = (d, right, left, far)

        def need(step):
            b = order[step]

            @pl.when(s == l)
            def _():
                if step == 0:
                    for i, (_, kept) in enumerate(expert_args):
                        arrived(kept.at[l, d], e_recv.at[i, l, d])
                if step == 3:
                    for i, (_, kept) in enumerate(expert_args):
                        arrived(kept.at[l, far], e_recv.at[i, l, far])
                        expert_forward(i, 2).start()

            @pl.when(s != l)
            def _():
                for i, (_, kept) in enumerate(expert_args):
                    arrived(kept.at[l, b], e_recv.at[i, l, b])

        need(0)
        need(1)
        pre = nn(rows_in[l], wi[l, d])
        for step in range(dps):
            if step + 1 < dps:
                if step:
                    need(step + 1)
                later = nn(rows_in[l], wi[l, order[step + 1]])
            b = order[step]
            after, dslope = gelu_parts(pre)
            after = after.astype(BF16)
            hidden[l, b] = after
            slope[l, b] = dslope.astype(BF16)
            term = nn(after, wu[l, b])
            acc[...] = term if step == 0 else acc[...] + term
            pre = later
        exchange_send(4 * l + 1, 0, acc[...])

    def slot_grads(l, way, grad_y, gate0, gate1):
        exchange_send(
            4 * l + 2, way,
            tn(s0[l], (gate0 * grad_y).astype(BF16)) + tn(s1[l], (gate1 * grad_y).astype(BF16)),
        )

    def expert_backward_pass(l, way):
        grows[...] = exchange_recv(4 * l + 2, way)
        acc[...] = jnp.zeros_like(acc)

        def block(b):
            before = (nt(grows[...], wu[l, b]) * slope[l, b].astype(F32)).astype(BF16)
            slope[l, b] = before
            acc[...] += nt(before, wi[l, b])
        for b in range(dps):
            block(b)
        exchange_send(4 * l + 3, way, acc[...])

    def part_copy(b, k):
        return remote(part.at[b, k], part_in.at[b, k], g_send.at[b, k], g_recv.at[b, k], twin)

    def expert_weights(l):
        def block(step):
            turn = 2 + step - 3 * (step // 2) - 2 * (step // 3)
            b, c = around(turn), around(dps - turn)
            part[b, 0] = tn(rows_in[l], slope[l, b]).astype(BF16)

            @pl.when(s != l)
            def _():
                part_copy(b, 0).start()

            part[c, 1] = tn(hidden[l, c], grows[...]).astype(BF16)

            @pl.when(s != l)
            def _():
                part_copy(c, 1).start()
        each(0, dps, block)

    def pair_part(b, k):
        arrived(part_in.at[b, k], g_recv.at[b, k])
        return part[b, k].astype(F32) + part_in[b, k].astype(F32)

    def ring_copy(k):
        return remote(
            part_in.at[far, k], ring.at[k], h_send.at[k], h_recv.at[k], (to_right, to_left)[k]
        )

    def ring_last(way, k):
        return remote(
            part_in.at[(right, left)[way], k], ring_end.at[way, k], k_send.at[way, k],
            k_recv.at[way, k], (to_right, to_left)[way],
        )

    def ring_first_step():
        for k in range(2):
            part_in[far, k] = pair_part(far, k).astype(BF16)
            ring_copy(k).start()
        for way, k in ((1, 0), (0, 1)):
            b = (right, left)[way]
            part_in[b, k] = pair_part(b, k).astype(BF16)
            ring_last(way, k).start()

    def ring_second_step():
        for way in range(2):
            b = (right, left)[way]
            value = pair_part(b, way)
            arrived(ring.at[way], h_recv.at[way])
            part_in[b, way] = (value + ring[way].astype(F32)).astype(BF16)
            ring_last(way, way).start()

    def ring_own():
        for k in range(2):
            part_acc[k] = pair_part(d, k)

    def ring_sent():
        for k in range(2):
            ring_copy(k).wait_send()
            for way in range(2):
                ring_last(way, k).wait_send()

    def part_sent():
        def done(b):
            for k in range(2):
                part_copy(b, k).wait_send()
        each(0, dps, done)

    def dense_twin(b):
        return remote(dense.at[b], dense_in.at[b], d_send.at[b], d_recv.at[b], twin)

    def dense_dp_copy(j):
        return remote(
            dense_in.at[around(j)], dense_dp.at[j - 1], dx_send.at[j - 1], dx_recv.at[j - 1],
            (s, e, around(j)),
        )

    def second_twin():
        return remote(second, second_in, d_send.at[dps], d_recv.at[dps], twin)

    def third_twin():
        return remote(third, third_in, d_send.at[dps + 1], d_recv.at[dps + 1], twin)

    def second_dp_copy(j):
        return remote(
            second_out.at[around(j)], second_last.at[d], sx_send.at[j - 1], sx_recv,
            (s, e, around(j)),
        )

    def narrow(values):
        half_width = values.shape[-1] // 2
        return jnp.concatenate(
            [values[:, :, :half_width], values[:, :, half_width:]], axis=1
        ).astype(BF16)

    def widen(values):
        return jnp.concatenate([values[:rows_own], values[rows_own:]], axis=1)

    def pair_rows(own, other, ends, send, recv):
        rows = rows_own * dps

        def pair(j):
            at = pl.ds(pl.multiple_of(j * rows, rows), rows)
            other[at] = (own[at].astype(F32) + other[at].astype(F32)).astype(BF16)
        each(0, experts, pair)
        for y, z in OFFSETS:
            peer = expert_at(y, z)
            at = pl.ds(pl.multiple_of(peer * rows, rows), rows)
            remote(other.at[at], ends.at[e], send, recv, (s, peer, d)).start()
        at = pl.ds(pl.multiple_of(e * rows, rows), rows)
        pltpu.make_async_copy(other.at[at], ends.at[e], recv).start()

    def pair_third():
        arrived(third_in, d_recv.at[dps + 1])
        pair_rows(third, third_in, third_far, ty_send, ty_recv)

    def pair_second():
        arrived(second_in, d_recv.at[dps])
        pair_rows(second, second_in, second_far, sy_send, sy_recv)

    def pair_first():
        for j in (2, 1, 3):
            other = around(j)
            arrived(dense_in.at[other], d_recv.at[other])
            dense_in[other] = (
                dense[other].astype(F32) + dense_in[other].astype(F32)
            ).astype(BF16)
            dense_dp_copy(j).start()
        arrived(dense_in.at[d], d_recv.at[d])
        dense_acc[...] = dense[d].astype(F32) + dense_in[d].astype(F32)

    def dense_middle():
        for j in (1, 3, 2):
            copy = dense_dp_copy(j)
            copy.wait_send()
            copy.wait_recv()
        summed = dense_acc[...]
        for j in range(dps - 1):
            summed = summed + dense_dp[j].astype(F32)
        dense_out[...] = narrow(summed.reshape(experts, rows_own, first_width))
        for y, z in OFFSETS:
            peer = expert_at(y, z)
            remote(
                dense_out.at[peer], dense_last.at[e], dy_send, dy_recv, (s, peer, d)
            ).start()
        pltpu.make_async_copy(dense_out.at[e], dense_last.at[e], dy_recv).start()
        arrived(third_far, ty_recv)
        arrived(third_in.at[pl.ds(0, features - rows_own * dps)], ty_send)
        late = third_far[0].astype(F32)
        for j in range(1, experts):
            late = late + third_far[j].astype(F32)
        arrived(second_far, sy_recv)
        arrived(second_in.at[pl.ds(0, features - rows_own * dps)], sy_send)
        summed = second_far[0].astype(F32)
        for j in range(1, experts):
            summed = summed + second_far[j].astype(F32)
        summed = jnp.concatenate([summed, late], axis=1)
        second_out[...] = narrow(summed.reshape(dps, rows_own, summed.shape[1]))
        for j in (2, 1, 3):
            second_dp_copy(j).start()
        pltpu.make_async_copy(second_out.at[d], second_last.at[d], sx_recv).start()

    def put(values, at):
        size = values.shape[1]
        blocks = values.reshape(experts, dps, rows_own, size)
        for b in range(dps):
            dense[b, :, pl.ds(at, size)] = blocks[:, b].reshape(rows_dp, size).astype(BF16)

    def put_extra(l):
        high, low = split_sum(small[l])
        lane = iota((8, EXTRA), 1)
        line = iota((8, EXTRA), 0)
        column = jnp.where((lane == line + experts) & (line < 4), 1.0, 0.0).astype(BF16)
        put(extra_kept[l] + tn(high, column) + tn(low, column), query_width)

    def put_third(l):
        third[...] = tn(blended[l], branch_kept[...]).astype(BF16)

        @pl.when(s != l)
        def _():
            third_twin().start()

    def put_second(l):
        second[:, :rest_width] = tn(norm1[l], gpacked[:, query_width:]).astype(BF16)

        @pl.when(s != l)
        def _():
            second_twin().start()

    def put_first(l):
        put(tn(norm1[l], gpacked[:, :query_width]), 0)
        put_extra(l)

        @pl.when(s != l)
        def _():
            for j in (2, 1, 3, 0):
                dense_twin(around(j)).start()

    def dense_twin_sent():
        third_twin().wait_send()
        second_twin().wait_send()
        for b in range(dps):
            dense_twin(b).wait_send()

    def gate_back(l, grad_y, gates):
        p, hit0, hit1, inverse, gate0, gate1 = gates
        gg0 = jnp.sum(grad_y * pick0[l].astype(F32), axis=1, keepdims=True)
        gg1 = jnp.sum(grad_y * pick1[l].astype(F32), axis=1, keepdims=True)
        mixed = gate0 * gg0 + gate1 * gg1
        q = (hit0 * (gg0 - mixed) + hit1 * (gg1 - mixed)) * inverse
        glog = p * (q - jnp.sum(p * q, axis=1, keepdims=True))
        high, low = split_sum(glog)
        extra_kept[l] = tn(norm2[l], high) + tn(norm2[l], low)
        return nn(high, wr128[l]) + nn(low, wr128[l])

    def attention_back(l, way, grad_y, from_gate, before, between):
        back = exchange_recv(4 * l + 3, way)
        grad_normed = nn(s0[l] + s1[l], back) + from_gate
        norm, root = normalized(attended[l])
        small[l, 0:1] = jnp.sum(grad_normed * norm, axis=0, keepdims=True)
        small[l, 1:2] = jnp.sum(grad_normed, axis=0, keepdims=True)
        grad_att = grad_y + norm_back(grad_normed, norm, root, gn[l, 1:2])
        branch = grad_att.astype(BF16)
        branch_kept[...] = branch
        before()
        gblend[...] = nt(branch, wo[l]).astype(BF16)
        for p in range(pairs):
            at = p * span
            queries = packed[l, :, at:at + span]
            keys = packed[l, :, features + at:features + at + span]
            values = packed[l, :, 2 * features + at:2 * features + at + span]
            prob = probs[l, p]
            low = prob.astype(BF16)
            grad_prob = jnp.concatenate([
                nt(
                    gblend[i * ROWS:(i + 1) * ROWS, at:at + span],
                    pair_keys(values[i * ROWS:(i + 1) * ROWS].astype(F32), lane_side),
                )
                for i in range(images)
            ], axis=0)
            mixed = prob * grad_prob
            sum0 = jnp.sum(jnp.where(in_left, mixed, 0.0), axis=-1, keepdims=True)
            sum1 = jnp.sum(jnp.where(in_left, 0.0, mixed), axis=-1, keepdims=True)
            grad_score = (prob * (grad_prob - jnp.where(in_left, sum0, sum1))).astype(BF16)
            for i in range(images):
                rows = slice(i * ROWS, (i + 1) * ROWS)
                one = grad_score[rows]
                grad_query = nn(one, pair_keys(keys[rows].astype(F32), lane_side)) * scale
                grad_key = tn(one, queries[rows]) * scale
                grad_value = tn(low[rows], gblend[rows, at:at + span])
                side = in_left[:ROWS]
                grad_key = jnp.where(side, grad_key[:ROWS], grad_key[ROWS:])
                grad_value = jnp.where(side, grad_value[:ROWS], grad_value[ROWS:])
                gpacked[rows, at:at + span] = grad_query.astype(BF16)
                gpacked[rows, features + at:features + at + span] = grad_key.astype(BF16)
                gpacked[rows, 2 * features + at:2 * features + at + span] = grad_value.astype(BF16)
        between()
        grad_normed = nt(gpacked[...], wq[l])
        norm, root = normalized(states[l].astype(F32))
        small[l, 2:3] = jnp.sum(grad_normed * norm, axis=0, keepdims=True)
        small[l, 3:4] = jnp.sum(grad_normed, axis=0, keepdims=True)
        return grad_att, grad_normed, norm, root

    def finish_back(l, grad_att, grad_normed, norm, root):
        gbuf[...] = (grad_att + norm_back(grad_normed, norm, root, gn[l, 0:1])).astype(BF16)

    def combine(l, gate0, gate1, way):
        back = exchange_recv(4 * l + 1, way)
        picked0 = nn(s0[l], back)
        picked1 = nn(s1[l], back)
        pick0[l] = picked0.astype(BF16)
        pick1[l] = picked1.astype(BF16)
        states[l + 1] = (attended[l] + gate0 * picked0 + gate1 * picked1).astype(BF16)

    route(0)
    attention(0)

    @pl.when(s == 0)
    def _():
        relay(0)
        relay_rest(0)

    route(1)
    expert_forward_pass(0)

    @pl.when(s == 1)
    def _():
        spread_experts()

    load_c.wait()
    gbuf[...] = nn(place[...], own_micro(cot)).astype(BF16)
    gates = gate_parts(0)
    combine(0, gates[4], gates[5], 0)

    @pl.when(s == 1)
    def _():
        relay(1)

    attention(1)
    gates = gate_parts(1)
    grad_y = gbuf[...].astype(F32)
    slot_grads(1, 1, grad_y, gates[4], gates[5])

    @pl.when(s == 1)
    def _():
        relay_rest(1)

    hand_out(0, 0, stage_out, states[1])
    expert_forward_pass(1)
    expert_backward_pass(1, 1)
    expert_weights(1)
    combine(1, gates[4], gates[5], 0)
    from_gate = gate_back(1, grad_y, gates)

    @pl.when(s == 1)
    def _():
        ring_first_step()

    kept = attention_back(1, 1, grad_y, from_gate, lambda: None, lambda: None)
    finish_back(1, *kept)

    gates = gate_parts(0)
    grad_y = gbuf[...].astype(F32)
    slot_grads(0, 0, grad_y, gates[4], gates[5])
    put_third(1)
    put_second(1)
    put_first(1)

    @pl.when(s == 1)
    def _():
        ring_second_step()
        ring_own()

    hand_out(0, 1, stage_out, states[2])
    hand_out(1, 1, stage_grad, gbuf[...])
    from_gate = gate_back(0, grad_y, gates)
    expert_backward_pass(0, 0)

    @pl.when(s == 0)
    def _():
        part_sent()

    expert_weights(0)

    @pl.when(s == 0)
    def _():
        ring_first_step()
        dense_twin_sent()

    @pl.when(s == 1)
    def _():
        pair_third()
        pair_second()
        pair_first()

    def between():
        put_second(0)

        @pl.when(s == 0)
        def _():
            ring_second_step()
            pair_third()
            pair_second()

    kept = attention_back(0, 0, grad_y, from_gate, lambda: put_third(0), between)
    put_first(0)

    @pl.when(s == 0)
    def _():
        pair_first()

    finish_back(0, *kept)
    hand_out(1, 0, stage_grad, gbuf[...])
    keep_out = join(0, stage_out, join_out, o_outs)
    keep_out.start()

    @pl.when(s == 0)
    def _():
        ring_own()

    dense_middle()

    for k in range(2):
        for way in range(2):
            arrived(ring_end.at[way, k], k_recv.at[way, k])
            part_acc[k] += ring_end[way, k].astype(F32)
    keep_in = pltpu.make_async_copy(part_acc.at[0], o_in, fin_sem.at[0])
    keep_up = pltpu.make_async_copy(part_acc.at[1], o_up, fin_sem.at[1])
    keep_in.start()
    keep_up.start()
    keep_grad = join(1, stage_grad, join_grad, o_grads)
    keep_grad.start()

    arrived(dense_last, dy_recv)
    arrived(second_last, sx_recv)
    final = jnp.concatenate([
        widen(jnp.sum(dense_last[...].astype(F32), axis=0)),
        widen(jnp.sum(second_last[...].astype(F32), axis=0)),
    ], axis=1)
    o_dense[...] = final
    tail = final[:, query_width:first_width]
    tail_high, tail_low = split_sum(tail)
    tail_low, tail_rest = split_sum(tail - tail_high.astype(F32))

    def column_rows(late, early):
        lane = iota((2, EXTRA), 1)
        line = iota((2, EXTRA), 0)
        wanted = jnp.where(line == 0, experts + early, experts + late)
        pick = jnp.where(lane == wanted, 1.0, 0.0).astype(BF16)
        return nt(pick, tail_high) + nt(pick, tail_low) + nt(pick, tail_rest)

    o_norms[0] = column_rows(0, 2)
    o_norms[1] = column_rows(1, 3)

    for i in range(5):
        dense_copy(i).wait_send()
    route_copy().wait_send()
    for i in range(2):
        expert_twin(i).wait_send()
        expert_relay(i).wait_send()
        for way in range(2):
            expert_next(i, way).wait_send()
        for j in range(1, dps):
            expert_forward(i, j).wait_send()

    ring_sent()

    @pl.when(s == 1)
    def _():
        part_sent()
        dense_twin_sent()

    out_copy(0, 1 - s, stage_out).wait_send()
    out_copy(1, 1 - s, stage_grad).wait_send()
    arrived(dense_out.at[pl.ds(0, experts - 1)], dy_send)
    for j in range(1, dps):
        second_dp_copy(j).wait_send()
    keep_out.wait()
    keep_grad.wait()
    keep_in.wait()
    keep_up.wait()


def finish(
    features, outs, grads, norms, dense, part_in, part_up,
    o_outs, o_grads, o_gain, o_bias, o_qkv, o_attn, o_router, o_in, o_up,
    v_in, v_up, v_outs, v_grads, sems,
):
    passes = (
        (part_in, v_in, o_in.at[0, 0]), (part_up, v_up, o_up.at[0, 0]),
        (outs, v_outs, o_outs), (grads, v_grads, o_grads),
    )
    loads = [
        pltpu.make_async_copy(source, kept, sems.at[0, i])
        for i, (source, kept, _) in enumerate(passes)
    ]
    copies = [
        pltpu.make_async_copy(kept, dest, sems.at[1, i])
        for i, (_, kept, dest) in enumerate(passes)
    ]
    for load in loads:
        load.start()
    o_gain[0] = norms[0]
    o_bias[0] = norms[1]
    width = dense.shape[-1]
    first = width * 2 // 9
    query = first - EXTRA
    o_qkv[0, :, :query] = dense[:, :query]
    o_qkv[0, :, query:] = dense[:, first: first + 3 * features - query]
    o_attn[0] = dense[:, width - features:]
    o_router[0] = dense[:, query: query + o_router.shape[-1]]
    for load, copy in zip(loads, copies):
        load.wait()
        copy.start()
    for copy in copies:
        copy.wait()


def local(
    dims, inputs, cotangent, gains, biases, w_qkv, w_out, w_router, w_in, w_up, routes
):
    sections, experts, dps, tokens, features, cap, ffs, micro = dims
    images = tokens // SEQ
    total = images * ROWS
    slots = experts * cap
    rows_dp = features // dps
    rows_own = rows_dp // experts
    width = -(-(4 * features + EXTRA) // 256) * 256
    first = width * 2 // 9
    second = width - first
    half = features // 2
    block = ffs // dps
    dma = pltpu.SemaphoreType.DMA
    anywhere = pl.BlockSpec(memory_space=pl.ANY)
    vmem = pl.BlockSpec(memory_space=pltpu.VMEM)

    def out(*shape, dtype=F32):
        return jax.ShapeDtypeStruct(shape, dtype)

    V = pltpu.VMEM
    pairs, span = HEADS // 2, 2 * HEAD_DIM
    scratch = [
        V((tokens, 2, features), BF16), V((tokens, 2, features), BF16),
        V((2, 2, tokens), jnp.int32),
        V((2, 2, features), F32), V((2, 2, features), F32),
        V((2, features, 3 * features), BF16), V((2, features, features), BF16),
        V((2, experts, features), BF16),
        V((2, dps, features, block), BF16), V((2, dps, block, features), BF16),
        V((total, tokens), BF16),
        V((2, total, slots), BF16), V((2, total, slots), BF16),
        V((2, total, EXTRA), F32), V((2, total, EXTRA), F32), V((2, EXTRA, features), BF16),
        V((3, total, features), BF16), V((2, total, features), BF16),
        V((2, total, 3 * features), BF16), V((2, pairs, total, span), F32),
        V((2, total, features), BF16), V((2, total, features), F32),
        V((2, total, features), BF16), V((2, total, EXTRA), F32),
        V((2, total, features), BF16), V((2, total, features), BF16),
        V((3, tokens, features), BF16), V((3, tokens, features), BF16),
        V((tokens, 2, features), BF16), V((tokens, 2, features), BF16),
        V((2, experts, 2 * cap, half), BF16), V((8, experts, 2 * cap, half), BF16),
        V((2, slots, features), BF16),
        V((2, dps, slots, block), BF16), V((2, dps, slots, block), BF16),
        V((slots, features), F32), V((slots, features), BF16),
        V((total, features), BF16), V((total, features), BF16), V((total, features), BF16),
        V((total, 3 * features), BF16),
        V((2, 8, features), F32), V((2, features, EXTRA), F32),
        V((dps, 2, features, block), BF16), V((dps, 2, features, block), BF16),
        V((2, features, block), F32), V((2, features, block), BF16),
        V((2, 2, features, block), BF16),
        V((dps, rows_dp, first), BF16), V((dps, rows_dp, first), BF16),
        V((rows_dp, first), F32), V((dps - 1, rows_dp, first), BF16),
        V((experts, 2 * rows_own, first // 2), BF16), V((experts, 2 * rows_own, first // 2), BF16),
        V((features, second - features), BF16), V((features, second - features), BF16),
        V((experts, dps * rows_own, second - features), BF16),
        V((dps, 2 * rows_own, second // 2), BF16), V((dps, 2 * rows_own, second // 2), BF16),
        V((features, features), BF16), V((features, features), BF16),
        V((experts, dps * rows_own, features), BF16),
        dma((2,)), dma((6,)), dma((2, 6)), dma((2, 2)), dma((2, 2, dps)), dma((2,)),
        dma((2, dps - 1)), dma((2,)),
        dma((2,)), dma((8,)), dma((2,)), dma((2,)), dma((2,)),
        dma((dps, 2)), dma((dps, 2)), dma((2,)), dma((2,)), dma((2, 2)), dma((2, 2)),
        dma((dps + 2,)), dma((dps + 2,)), dma((dps - 1,)), dma((dps - 1,)), dma, dma, dma, dma,
        dma((dps - 1,)), dma, dma, dma, dma((2,)),
    ]
    made = pl.pallas_call(
        partial(kernel, dims),
        out_shape=(
            out(tokens, micro, features, dtype=BF16),
            out(tokens, micro, features, dtype=BF16),
            out(2, 2, rows_own),
            out(rows_own, width),
            out(features, block),
            out(block, features),
        ),
        in_specs=[anywhere, anywhere, vmem, vmem, anywhere, anywhere, vmem, anywhere, anywhere, vmem],
        out_specs=(anywhere, anywhere, vmem, vmem, anywhere, anywhere),
        scratch_shapes=scratch,
        compiler_params=pltpu.CompilerParams(
            collective_id=0, has_side_effects=True, vmem_limit_bytes=62 * 2**20
        ),
        cost_estimate=pl.CostEstimate(
            flops=10_000_000_000, bytes_accessed=10_000_000, transcendentals=4_000_000
        ),
    )(
        inputs.transpose(1, 0, 2), cotangent.transpose(1, 0, 2), gains, biases, w_qkv, w_out,
        w_router.transpose(0, 2, 1), w_in, w_up, routes.transpose(0, 1, 3, 2),
    )
    outs, grads, *rest = pl.pallas_call(
        partial(finish, features),
        out_shape=(
            out(tokens, micro, features, dtype=BF16),
            out(tokens, micro, features, dtype=BF16),
            out(1, 2, rows_own),
            out(1, 2, rows_own),
            out(1, rows_own, 3 * features),
            out(1, rows_own, features),
            out(1, rows_own, experts),
            out(1, 1, features, block),
            out(1, 1, block, features),
        ),
        in_specs=[anywhere, anywhere, vmem, vmem, anywhere, anywhere],
        out_specs=(anywhere, anywhere, vmem, vmem, vmem, vmem, vmem, anywhere, anywhere),
        scratch_shapes=[
            V((features, block), F32), V((block, features), F32),
            V((tokens, micro, features), BF16), V((tokens, micro, features), BF16), dma((2, 4)),
        ],
    )(*made)
    return (
        outs.transpose(1, 0, 2)[None],
        grads.transpose(1, 0, 2)[None],
        *rest,
    )


def solution(mesh):
    sections, experts, dps = (mesh.shape[name] for name in ("section", "expert", "dp"))

    def run(*args):
        tokens, features = args[0].shape[1:]
        micro = args[0].shape[0]
        cap = 5 * tokens // (2 * experts) + 1
        ffs = args[7].shape[3] * dps
        dims = (sections, experts, dps, tokens, features, cap, ffs, micro)
        return local(dims, *args)

    return jax.shard_map(
        run,
        mesh=mesh,
        in_specs=(
            P(None, ("expert", "dp"), None),
            P(None, ("expert", "dp"), None),
            P("section", None, None),
            P("section", None, None),
            P("section", None, None),
            P("section", None, None),
            P("section", None, None),
            P("section", "expert", None, "dp"),
            P("section", "expert", "dp", None),
            P("section", None, ("expert", "dp"), None),
        ),
        out_specs=(
            P("section", None, ("expert", "dp"), None),
            P("section", None, ("expert", "dp"), None),
            P("section", None, ("expert", "dp")),
            P("section", None, ("expert", "dp")),
            P("section", ("expert", "dp"), None),
            P("section", ("expert", "dp"), None),
            P("section", ("expert", "dp"), None),
            P("section", "expert", None, "dp"),
            P("section", "expert", "dp", None),
        ),
        check_vma=False,
    )
```
